256 devices in a mesh: dp: 8 (over y, z_hi), ctx: 32 (over z_lo, x, core).
Axes of the slice: x: 4, y: 4, z: 8 (z_hi: 2, z_lo: 4; z = z_hi * 4 + z_lo), core: 2. Of those that a mesh axis runs over, the one named last changes fastest.
Arguments:
- hidden_state: bfloat16 [8, 32768, 1536], P('dp', 'ctx'), may hold values from -45 to 45
- tokens: int32 [8, 32768], P('dp', 'ctx'), may hold values from 0 to 4
- in_codes: bfloat16 [24, 32, 1536], P('dp'), may hold values from -0.21875 to 0.21875
- in_scales: float32 [24, 12], P('dp'), may hold values from 0.5 to 2
- out_codes: bfloat16 [24, 32, 768], P('dp'), may hold values from -0.21875 to 0.21875
- out_scales: float32 [24, 6], P('dp'), may hold values from 0.5 to 2
- short_filter: bfloat16 [4, 768], replicated, may hold values from -3 to 3
- long_filter: bfloat16 [128, 768], replicated, may hold values from -0.5 to 0.5
Outputs:
- new_state: bfloat16 [8, 32768, 1536], P('dp', 'ctx')
The draws below stay inside these ranges and needn't reach their ends.
Inputs may be any that keep to these rules, and one draw needn't show every extreme that they name: `tokens`: values 0 to 3 are the bases A, C, G, T; 4 is an unknown base N.
All inputs are finite; a program needn't handle non-finite values.
Results may differ from the reference program's by a relative error of at most 0.022.
Values may be sent and summed in bfloat16 or wider, within the bound.
A program may use at most 128 MiB of HBM per device.

```python
import math
import jax
import jax.numpy as jnp
from jax import lax

D = 1536
H = 768
E = 768
SEQ = 32768
BATCH = 8
SHORT_TAPS = 4
LONG_TAPS = 128
SCALE_ROWS = 32
SCALE_COLS = 128


def draw_hidden_state(key, part):
    key = jax.random.fold_in(key, 11)
    key_base, key_rows, key_cols = jax.random.split(key, 3)
    row_scale = jnp.exp(jax.random.uniform(key_rows, (BATCH, SEQ, 1), jnp.float32, math.log(0.25), math.log(2.5)))
    col_scale = jnp.exp(jax.random.uniform(key_cols, (1, 1, D), jnp.float32, math.log(0.3), math.log(3.0)))
    base = jnp.clip(jax.random.normal(key_base, (BATCH, SEQ, D), jnp.float32), -6.0, 6.0)
    return (base * row_scale * col_scale).astype(jnp.bfloat16)


def set_ends(entries, own_key, smallest, largest):
    index_at = [jax.random.randint(jax.random.fold_in(own_key, axis), (), 0, length) for axis, length in enumerate(entries.shape)]
    widest = entries.shape.index(max(entries.shape))
    beside = index_at[:widest] + [(index_at[widest] + 1) % entries.shape[widest]] + index_at[widest + 1:]
    return entries.at[tuple(index_at)].set(smallest).at[tuple(beside)].set(largest)


def steps_of(own_key, dims, shards, least, largest):
    factor_of = 1.0
    for position, blocks in shards:
        draws = jax.random.uniform(jax.random.fold_in(jax.random.fold_in(own_key, 6), position), (blocks,), jnp.float32, least / len(shards), largest / len(shards))
        factor_of = factor_of * jnp.repeat(jnp.exp(draws), dims[position] // blocks).reshape((-1,) + (1,) * (len(dims) - 1 - position))
    return factor_of


def noise(stream_key, dims, width, limit, cuts=(), dtype=jnp.bfloat16):
    drawn = width * jax.random.normal(stream_key, dims, jnp.float32)
    if cuts:
        drawn = drawn * steps_of(stream_key, dims, cuts, -0.22, 0.18)
    return jnp.clip(drawn, -limit, limit).astype(dtype)


def setup_inputs(seed: int = 0) -> dict:
    key_of = jax.random.split(jax.random.key(seed), 9)
    return {
        "hidden_state": draw_hidden_state(jax.random.fold_in(key_of[8], 71), 0),
        "tokens": set_ends(jax.random.randint(key_of[1], (BATCH, SEQ), 0, 5), jax.random.fold_in(key_of[1], 1), 0, 4).astype(jnp.int32),
        "in_codes": noise(key_of[2], (H // SCALE_ROWS, SCALE_ROWS, 2 * E), H ** -0.5, 0.21875, ((0, 8),)),
        "in_scales": jnp.clip(jnp.exp(math.log(2.0) - 1.3862944 * jax.random.uniform(key_of[3], (H // SCALE_ROWS, 2 * E // SCALE_COLS), jnp.float32) ** steps_of(key_of[3], (H // SCALE_ROWS, 2 * E // SCALE_COLS), ((0, 8),), -0.2, 0.2)), 0.5, 2.0),
        "out_codes": noise(key_of[4], (E // SCALE_ROWS, SCALE_ROWS, H), E ** -0.5, 0.21875, ((0, 8),)),
        "out_scales": jnp.clip(jnp.exp(math.log(2.0) - 1.3862944 * jax.random.uniform(key_of[5], (E // SCALE_ROWS, H // SCALE_COLS), jnp.float32) ** steps_of(key_of[5], (E // SCALE_ROWS, H // SCALE_COLS), ((0, 8),), -0.2, 0.2)), 0.5, 2.0),
        "short_filter": noise(key_of[6], (SHORT_TAPS, E), SHORT_TAPS ** -0.5, 3.0),
        "long_filter": noise(key_of[7], (LONG_TAPS, E), LONG_TAPS ** -0.5, 0.5),
    }


def dequantize(codes, scales):
    widened = jnp.repeat(scales, SCALE_COLS, axis=1)[:, None, :]
    weight = (codes.astype(jnp.float32) * widened).astype(jnp.bfloat16)
    return weight.reshape(codes.shape[0] * codes.shape[1], codes.shape[2])

def causal_taps(values, filter_taps):
    tap_count = filter_taps.shape[0]
    length = values.shape[1]
    padded = jnp.pad(values.astype(jnp.float32), ((0, 0), (tap_count - 1, 0), (0, 0)))
    weights = filter_taps.astype(jnp.float32)

    def accumulate(tap_index, running):
        window = lax.dynamic_slice_in_dim(padded, tap_index, length, 1)
        return running + window * weights[tap_index]
    return lax.fori_loop(0, tap_count, accumulate, jnp.zeros(values.shape, jnp.float32))

def reference(hidden_state, tokens, in_codes, in_scales, out_codes, out_scales, short_filter, long_filter):
    w_in = dequantize(in_codes, in_scales)
    w_out = dequantize(out_codes, out_scales)

    def one_window(operands):
        window_state, window_letters = operands
        forward = window_state[:, :H]
        backward = window_state[::-1, H:]
        forward_keep = (window_letters != 4).astype(jnp.float32)
        keep_mask = jnp.stack([forward_keep, forward_keep[::-1]])
        strands = jnp.stack([forward, backward])
        widened = strands.astype(jnp.float32)
        normed = (widened * lax.rsqrt(lax.optimization_barrier(jnp.mean(widened * widened, axis=-1, keepdims=True)) + 1e-05)).astype(jnp.bfloat16)
        projected = jnp.dot(normed.reshape(2 * SEQ, H), w_in, preferred_element_type=jnp.float32).reshape(2, SEQ, 2 * E)
        masked = (projected[:, :, :E] * keep_mask[:, :, None]).astype(jnp.bfloat16)
        gate_part = projected[:, :, E:]
        short_out = causal_taps(masked, short_filter).astype(jnp.bfloat16)
        long_out = causal_taps(short_out, long_filter)
        gated = (jax.nn.silu(gate_part) * long_out).astype(jnp.bfloat16)
        branch = jnp.dot(gated.reshape(2 * SEQ, E), w_out, preferred_element_type=jnp.float32).reshape(2, SEQ, H)
        forward_out = (forward.astype(jnp.float32) + branch[0]).astype(jnp.bfloat16)
        backward_out = (backward.astype(jnp.float32) + branch[1]).astype(jnp.bfloat16)[::-1]
        return jnp.concatenate([forward_out, backward_out], axis=-1)
    return lax.map(one_window, (hidden_state, tokens))
```

```python
import functools

import jax
import jax.numpy as jnp
import numpy as np
from jax import lax
from jax.experimental import pallas as pl
from jax.experimental.pallas import tpu as pltpu
from jax.sharding import PartitionSpec as P

MESH = pl.DeviceIdType.MESH
F32, BF16 = jnp.float32, jnp.bfloat16
ROWS, HALO = 1024, 144
WIDTH, SHARD = 768, 96
BLOCK, SPAN = 128, 256
TILE = 256
DP, CTX = 8, 32
LONG, SHORT = 128, 4
VMEM_LIMIT = 63 << 20


def transform(positions):
    freq = np.arange(BLOCK)[:, None]
    angle = 2 * np.pi * ((freq * positions[None, :]) % SPAN) / SPAN
    real, imag = np.cos(angle), -np.sin(angle)
    imag[0] = np.cos(np.pi * (positions % 2))
    return np.concatenate([real, imag], axis=0)


def split(matrix):
    high = matrix.astype(np.float32).astype(BF16)
    return high, (matrix - high.astype(np.float64)).astype(np.float32).astype(BF16)


def constants():
    spread = transform(np.arange(SPAN))
    long_high, long_low = split(transform(LONG - 1 - np.arange(LONG)))
    short_table = np.zeros((SPAN, 16))
    short_table[:, :SHORT] = transform(SHORT - 1 - np.arange(SHORT))
    short_high, short_low = split(short_table)
    as_bf16 = lambda table: table.astype(np.float32).astype(BF16)
    gather_forward = as_bf16(spread[:, BLOCK:].T)
    gather_backward = as_bf16(spread[:, :BLOCK].T)
    return (
        as_bf16(spread),
        gather_forward,
        gather_backward,
        long_high,
        long_low,
        short_high,
        short_low,
    )


def layer_kernel(
    hidden,
    tokens,
    in_codes,
    in_scales,
    out_codes,
    out_scales,
    short_source,
    long_source,
    spread_source,
    gather_forward_source,
    gather_backward_source,
    long_high_source,
    long_low_source,
    short_high_source,
    short_low_source,
    out,
    weights,
    codes,
    last_codes,
    scales,
    last_scales,
    letters,
    token_forward,
    token_backward,
    halo_forward,
    halo_backward,
    short_filter,
    long_filter,
    spread,
    gather_forward,
    gather_backward,
    long_high,
    long_low,
    short_high,
    short_low,
    state,
    normed,
    masked_forward,
    masked_backward,
    keep,
    pure,
    cross,
    edge,
    taps,
    conv,
    load_sem,
    store_sem,
    piece_recv,
    cross_recv,
    mate_recv,
    halo_recv,
    z_send,
    y_send,
    x_send,
    mate_send,
    halo_send,
):
    dp, ctx = lax.axis_index("dp"), lax.axis_index("ctx")
    y, z_high = dp // 2, dp % 2
    z_low, x, core = ctx // 8, (ctx // 2) % 4, ctx % 2
    half = x % 2
    partner = dp + 1 - 2 * z_high
    ring = 4
    below, above, across = (y + 3) % ring, (y + 1) % ring, (y + 2) % ring
    up, down = ((dp + 2) % DP, ctx), ((dp + DP - 2) % DP, ctx)
    opposite = ((dp + 4) % DP, ctx)
    step = 1 - 2 * core
    beside = (dp, z_low * 8 + (x + ring + step) % ring * 2 + core)
    beside_source = (dp, z_low * 8 + (x + ring - step) % ring * 2 + core)
    mate = (dp, ctx + step)
    after, before = (dp, (ctx + 1) % CTX), (dp, (ctx + CTX - 1) % CTX)
    border = z_low // 3 + (3 - z_low) // 3
    fetches = (core + z_high) % 2

    loads = []

    def load(source, target):
        index = len(loads)
        copy = pltpu.make_async_copy(source, target, load_sem.at[index])
        copy.start()
        loads.append(copy)
        return copy

    code_loads = [load(in_codes, codes), load(in_scales, scales)]
    last_loads = [load(out_codes, last_codes), load(out_scales, last_scales)]
    letter_load = load(tokens, letters)
    filter_loads = [
        load(short_source, short_filter),
        load(long_source, long_filter),
        load(long_high_source, long_high),
        load(long_low_source, long_low),
        load(short_high_source, short_high),
        load(short_low_source, short_low),
    ]
    state_loads = [
        load(hidden.at[:, pl.ds(strand * WIDTH, WIDTH)], state.at[strand]) for strand in range(2)
    ]
    table_loads = [
        load(spread_source, spread),
        load(gather_forward_source, gather_forward),
        load(gather_backward_source, gather_backward),
    ]

    barrier = pltpu.get_barrier_semaphore()
    for device in (up, down, opposite, beside_source, mate, after, before):
        pl.semaphore_signal(barrier, inc=1, device_id=device, device_id_type=MESH)

    @pl.when(fetches == 1)
    def _():
        shift = (z_low // 2) * 24
        source = (partner, ctx + 24 - 8 * z_low - shift)
        pl.semaphore_signal(barrier, inc=1, device_id=source, device_id_type=MESH)

    def dequantise(part):
        for block in range(3):
            rows = pl.ds(pl.multiple_of(dp * SHARD + block * 32, 32), 32)
            for group in range(6):
                column = group * 128
                if part < 2:
                    place = part * 6 + group
                    values = codes[block, :, place * 128 : place * 128 + 128]
                    scale = scales[block : block + 1, place : place + 1]
                else:
                    values = last_codes[block, :, column : column + 128]
                    scale = last_scales[block : block + 1, group : group + 1]
                weights[part, rows, column : column + 128] = (values.astype(F32) * scale).astype(BF16)

    for copy in code_loads:
        copy.wait()
    dequantise(0)
    pl.semaphore_wait(barrier, 7 + 2 * border * (1 - fetches))

    def rows_of(row, side):
        return pl.ds(pl.multiple_of((2 * row + side) * SHARD, 32), SHARD)

    def piece(part, row, side):
        start = (2 * row + core) * SHARD + side * (SHARD // 2)
        return weights.at[part, pl.ds(pl.multiple_of(start, 16), SHARD // 2)]

    def remote(ref, device, sent, received):
        return pltpu.make_async_remote_copy(
            src_ref=ref,
            dst_ref=ref,
            send_sem=sent,
            recv_sem=received,
            device_id=device,
            device_id_type=MESH,
        )

    def along(part, row, device, index):
        return remote(
            piece(part, row, half), device, y_send.at[part, index], piece_recv.at[part, row]
        )

    def aside(part, row, index):
        return remote(
            piece(part, row, half), beside, x_send.at[part, index], cross_recv.at[part, row]
        )

    def to_mate(part, row, index):
        ref = weights.at[part, rows_of(row, core)]
        return remote(ref, mate, mate_send.at[part, index], mate_recv.at[part, row])

    def z_copies(part):
        sign = 1 - 2 * (z_low // 3)
        return [
            remote(
                piece(part, y, half),
                (partner, ctx + distance * sign),
                z_send.at[part, index],
                piece_recv.at[part, y],
            )
            for index, distance in enumerate((16, 24))
        ]

    def ring_copies(part):
        return [along(part, y, up, 0), along(part, y, down, 1), along(part, y, opposite, 2)]

    def owner(part, action):
        @pl.when(fetches == 0)
        def _():
            @pl.when(border == 1)
            def _():
                for copy in z_copies(part):
                    action(copy)

            for copy in ring_copies(part):
                action(copy)

    def start(copy):
        copy.start()

    def open_part(part):
        owner(part, start)

    def relay(part):
        @pl.when(fetches == 1)
        def _():
            along(part, y, up, 0).wait_recv()
            for copy in ring_copies(part):
                copy.start()
            aside(part, y, 0).start()

    def collect(part):
        for index, row in enumerate((below, above, across)):
            along(part, row, up, 0).wait_recv()
            aside(part, row, index + 1).start()

    def share(part):
        @pl.when(fetches == 1)
        def _():
            remote(
                piece(part, y, 1 - half), beside, x_send.at[part, 0], cross_recv.at[part, y]
            ).wait_recv()
            to_mate(part, y, 0).start()

        for index, row in enumerate((below, above, across)):
            remote(
                piece(part, row, 1 - half), beside, x_send.at[part, 0], cross_recv.at[part, row]
            ).wait_recv()
            to_mate(part, row, index + 1).start()

    def complete(part):
        def finish(row):
            ref = weights.at[part, rows_of(row, 1 - core)]
            remote(ref, mate, mate_send.at[part, 0], mate_recv.at[part, row]).wait_recv()

        @pl.when(fetches == 0)
        def _():
            finish(y)

        for row in (below, above, across):
            finish(row)

    halos = []

    def halo(source, target, device):
        index = len(halos)
        copy = pltpu.make_async_remote_copy(
            src_ref=source,
            dst_ref=target,
            send_sem=halo_send.at[index],
            recv_sem=halo_recv.at[index],
            device_id=device,
            device_id_type=MESH,
        )
        copy.start()
        halos.append(copy)

    open_part(0)
    for copy in last_loads:
        copy.wait()
    dequantise(1)
    dequantise(2)
    letter_load.wait()
    halo(letters.at[:, pl.ds(ROWS - 256, 256)], token_forward, after)
    halo(letters.at[:, pl.ds(0, 256)], token_backward, before)
    halo(hidden.at[pl.ds(ROWS - HALO, HALO), pl.ds(0, WIDTH)], halo_forward, after)
    halo(hidden.at[pl.ds(0, HALO), pl.ds(WIDTH, WIDTH)], halo_backward, before)
    for copy in filter_loads:
        copy.wait()
    short = short_filter[...].astype(F32)
    long = long_filter[...]
    padded = jnp.concatenate([short, jnp.zeros((16 - SHORT, WIDTH), F32)], axis=0).astype(BF16)
    dot = functools.partial(jnp.dot, preferred_element_type=F32)
    long_hat = dot(long_high[...], long) + dot(long_low[...], long)
    short_hat = dot(short_high[...], padded) + dot(short_low[...], padded)
    real_long, imag_long = long_hat[:BLOCK], long_hat[BLOCK:]
    real_short, imag_short = short_hat[:BLOCK], short_hat[BLOCK:]
    first = lax.broadcasted_iota(jnp.int32, (BLOCK, WIDTH), 0) == 0
    scale = jnp.where(first, 1.0 / SPAN, 2.0 / SPAN)
    reals, imags = real_short * real_long, imag_short * imag_long
    pure[...] = jnp.where(first, reals, reals - imags) * scale
    edge[...] = jnp.where(first, imags, reals - imags) * scale
    cross[...] = jnp.where(first, 0.0, real_short * imag_long + imag_short * real_long) * scale
    long_head = long[:16].astype(F32)
    taps[0:1] = short[0:1] * long_head[0:1]
    taps[1:2] = short[0:1] * long_head[1:2] + short[1:2] * long_head[0:1]

    relay(0)
    open_part(1)
    open_part(2)

    def keep_rows(values, live):
        flags = jnp.where(values != 4, live, 0.0)
        return jnp.transpose(jnp.broadcast_to(flags, (128, 128)))

    one = jnp.float32(1.0)
    for block in range(ROWS // 128):
        keep[block * 128 + 256 : block * 128 + 384] = keep_rows(
            letters[:, block * 128 : block * 128 + 128], one
        )

    def project(values):
        wide = values.astype(F32)
        mean = jnp.mean(wide * wide, axis=-1, keepdims=True)
        return (wide * lax.rsqrt(mean + 1e-5)).astype(BF16)

    for copy in state_loads:
        copy.wait()

    def norm_pass(tile, carry):
        rows = pl.ds(pl.multiple_of(tile * TILE, TILE), TILE)
        for strand in range(2):
            normed[strand, rows] = project(state[strand, rows])
        return carry

    lax.fori_loop(0, 2, norm_pass, 0)
    collect(0)
    relay(1)
    relay(2)
    lax.fori_loop(2, ROWS // TILE, norm_pass, 0)
    for copy in table_loads:
        copy.wait()
    share(0)
    collect(1)
    complete(0)

    def value_part(norm, flags):
        return (dot(norm, weights[0]) * jnp.tile(flags, (1, 6))).astype(BF16)

    def value_pass(tile, carry):
        start = pl.multiple_of(tile * TILE, TILE)
        rows = pl.ds(start, TILE)
        flags = keep[pl.ds(start + 256, TILE)]
        masked_forward[pl.ds(pl.multiple_of(start + HALO, 16), TILE)] = value_part(
            normed[0, rows], flags
        )
        masked_backward[rows] = value_part(normed[1, rows], flags)
        return carry

    lax.fori_loop(0, 2, value_pass, 0)
    collect(2)
    share(1)
    lax.fori_loop(2, ROWS // TILE, value_pass, 0)

    for copy in halos:
        copy.wait_recv()
    live_before = jnp.where(ctx > 0, 1.0, 0.0)
    live_after = jnp.where(ctx < CTX - 1, 1.0, 0.0)
    for block in range(2):
        columns = slice(block * 128, block * 128 + 128)
        keep[columns] = keep_rows(token_forward[:, columns], live_before)
        keep[ROWS + 256 + block * 128 : ROWS + 384 + block * 128] = keep_rows(
            token_backward[:, columns], live_after
        )
    masked_forward[0:HALO] = value_part(project(halo_forward[...]), keep[256 - HALO : 256])
    masked_backward[ROWS : ROWS + HALO] = value_part(
        project(halo_backward[...]), keep[ROWS + 256 : ROWS + 256 + HALO]
    )
    share(2)
    complete(1)

    def filtered(strand, start, target):
        masked = masked_backward if strand else masked_forward
        origin = start if strand else pl.multiple_of(start + 16, 16)
        window = masked[pl.ds(origin, SPAN)]
        waves = dot(spread[...], window)
        real, imag = waves[:BLOCK], waves[BLOCK:]
        straight, turned = real * pure[...], imag * cross[...]
        upright, bent = imag * edge[...], real * cross[...]
        if strand:
            parts = [straight + turned, upright - bent]
        else:
            parts = [straight - turned, upright + bent]
        product = jnp.concatenate([part.astype(BF16) for part in parts], axis=0)
        gather = gather_backward if strand else gather_forward
        conv[target : target + BLOCK] = dot(gather[...], product)
        last, second = taps[0:1], taps[1:2]
        row = lax.broadcasted_iota(jnp.int32, (8, WIDTH), 0)
        if strand:
            wrong = masked[pl.ds(start, 16)].astype(F32)
            right = masked[pl.ds(pl.multiple_of(start + SPAN, 16), 16)].astype(F32)
            gap = right - wrong
            outer, inner = gap[0:1], gap[1:2]
            fix = jnp.where(row == 7, second * outer + last * inner, 0.0)
            fix = fix + jnp.where(row == 6, last * outer, 0.0)
            conv[target + BLOCK - 8 : target + BLOCK] += fix
        else:
            right = masked[pl.ds(start, 16)].astype(F32)
            wrong = masked[pl.ds(pl.multiple_of(start + SPAN, 16), 16)].astype(F32)
            gap = right - wrong
            outer, inner = gap[15:16], gap[14:15]
            fix = jnp.where(row == 0, second * outer + last * inner, 0.0)
            fix = fix + jnp.where(row == 1, last * outer, 0.0)
            conv[target : target + 8] += fix

    def gate_pass(tile, carry):
        start = pl.multiple_of(tile * TILE, TILE)
        rows = pl.ds(start, TILE)
        for strand in range(2):
            base = strand * TILE
            for block in range(TILE // BLOCK):
                filtered(strand, pl.multiple_of(start + block * BLOCK, BLOCK), base + block * BLOCK)
            gate = dot(normed[strand, rows], weights[1])
            half_gate = 0.5 * gate
            gated = (half_gate * jnp.tanh(half_gate) + half_gate) * conv[base : base + TILE]
            normed[strand, rows] = gated.astype(BF16)
        return carry

    lax.fori_loop(0, ROWS // TILE, gate_pass, 0)
    complete(2)

    def store(strand, start):
        rows = pl.ds(start, TILE)
        columns = pl.ds(strand * WIDTH, WIDTH)
        return pltpu.make_async_copy(
            state.at[strand, rows], out.at[rows, columns], store_sem.at[strand, start // TILE]
        )

    def out_pass(tile, carry):
        start = pl.multiple_of(tile * TILE, TILE)
        rows = pl.ds(start, TILE)
        for strand in range(2):
            branch = dot(normed[strand, rows], weights[2])
            state[strand, rows] = (state[strand, rows].astype(F32) + branch).astype(BF16)
            store(strand, start).start()
        return carry

    lax.fori_loop(0, ROWS // TILE, out_pass, 0)

    for copy in halos:
        copy.wait_send()
    for part in range(3):
        owner(part, lambda copy: copy.wait_send())

        @pl.when(fetches == 1)
        def _(part=part):
            for copy in ring_copies(part):
                copy.wait_send()
            aside(part, y, 0).wait_send()
            to_mate(part, y, 0).wait_send()

        for index, row in enumerate((below, above, across)):
            aside(part, row, index + 1).wait_send()
            to_mate(part, row, index + 1).wait_send()
    for strand in range(2):
        for tile in range(ROWS // TILE):
            store(strand, tile * TILE).wait()


def shards(
    hidden_state, tokens, in_codes, in_scales, out_codes, out_scales, short_filter, long_filter
):
    anywhere = pl.BlockSpec(memory_space=pl.ANY)
    dma = pltpu.SemaphoreType.DMA
    tables = constants()
    result = pl.pallas_call(
        layer_kernel,
        out_shape=jax.ShapeDtypeStruct((ROWS, 2 * WIDTH), BF16),
        in_specs=[anywhere] * (8 + len(tables)),
        out_specs=anywhere,
        scratch_shapes=[
            pltpu.VMEM((3, WIDTH, WIDTH), BF16),
            pltpu.VMEM((3, 32, 2 * WIDTH), BF16),
            pltpu.VMEM((3, 32, WIDTH), BF16),
            pltpu.VMEM((3, 12), F32),
            pltpu.VMEM((3, 6), F32),
            pltpu.VMEM((1, ROWS), jnp.int32),
            pltpu.VMEM((1, 256), jnp.int32),
            pltpu.VMEM((1, 256), jnp.int32),
            pltpu.VMEM((HALO, WIDTH), BF16),
            pltpu.VMEM((HALO, WIDTH), BF16),
            pltpu.VMEM((SHORT, WIDTH), BF16),
            pltpu.VMEM((LONG, WIDTH), BF16),
            *(pltpu.VMEM(table.shape, BF16) for table in tables),
            pltpu.VMEM((2, ROWS, WIDTH), BF16),
            pltpu.VMEM((2, ROWS, WIDTH), BF16),
            pltpu.VMEM((ROWS + HALO, WIDTH), BF16),
            pltpu.VMEM((ROWS + HALO, WIDTH), BF16),
            pltpu.VMEM((ROWS + 512, 128), F32),
            pltpu.VMEM((BLOCK, WIDTH), F32),
            pltpu.VMEM((BLOCK, WIDTH), F32),
            pltpu.VMEM((BLOCK, WIDTH), F32),
            pltpu.VMEM((8, WIDTH), F32),
            pltpu.VMEM((2 * TILE, WIDTH), F32),
            dma((16,)),
            dma((2, ROWS // TILE)),
            dma((3, 4)),
            dma((3, 4)),
            dma((3, 4)),
            dma((4,)),
            dma((3, 2)),
            dma((3, 3)),
            dma((3, 4)),
            dma((3, 4)),
            dma((4,)),
        ],
        compiler_params=pltpu.CompilerParams(
            collective_id=0, has_side_effects=True, vmem_limit_bytes=VMEM_LIMIT
        ),
        name="layer",
    )(
        hidden_state[0],
        tokens,
        in_codes,
        in_scales,
        out_codes,
        out_scales,
        short_filter,
        long_filter,
        *map(jnp.asarray, tables),
    )
    return result[None]


def solution(mesh):
    in_specs = (
        P("dp", "ctx", None),
        P("dp", "ctx"),
        P("dp", None, None),
        P("dp", None),
        P("dp", None, None),
        P("dp", None),
        P(),
        P(),
    )
    out_specs = P("dp", "ctx", None)
    return jax.shard_map(shards, mesh=mesh, in_specs=in_specs, out_specs=out_specs, check_vma=False)
```

```python
import functools

import jax
import jax.numpy as jnp
import numpy as np
from jax import lax
from jax.experimental import pallas as pl
from jax.experimental.pallas import tpu as pltpu
from jax.sharding import PartitionSpec as P

MESH = pl.DeviceIdType.MESH
F32, BF16 = jnp.float32, jnp.bfloat16
ROWS, HALO = 1024, 144
WIDTH, SHARD = 768, 96
BLOCK, SPAN = 128, 256
TILE, PART = 512, 256
DP, CTX = 8, 32
LONG, SHORT = 128, 4
VMEM_LIMIT = 63 << 20


def transform(positions):
    freq = np.arange(BLOCK)[:, None]
    angle = 2 * np.pi * ((freq * positions[None, :]) % SPAN) / SPAN
    real, imag = np.cos(angle), -np.sin(angle)
    imag[0] = np.cos(np.pi * (positions % 2))
    return np.concatenate([real, imag], axis=0)


def split(matrix):
    high = matrix.astype(np.float32).astype(BF16)
    return high, (matrix - high.astype(np.float64)).astype(np.float32).astype(BF16)


def constants():
    spread = transform(np.arange(SPAN))
    long_high, long_low = split(transform(LONG - 1 - np.arange(LONG)))
    short_table = np.zeros((SPAN, 16))
    short_table[:, :SHORT] = transform(SHORT - 1 - np.arange(SHORT))
    short_high, short_low = split(short_table)
    as_bf16 = lambda table: table.astype(np.float32).astype(BF16)
    gather_forward = as_bf16(spread[:, BLOCK:].T)
    gather_backward = as_bf16(spread[:, :BLOCK].T)
    return (
        as_bf16(spread),
        gather_forward,
        gather_backward,
        long_high,
        long_low,
        short_high,
        short_low,
    )


def layer_kernel(
    hidden,
    tokens,
    in_codes,
    in_scales,
    out_codes,
    out_scales,
    short_source,
    long_source,
    spread_source,
    gather_forward_source,
    gather_backward_source,
    long_high_source,
    long_low_source,
    short_high_source,
    short_low_source,
    gated_out,
    last_weights,
    weights,
    codes,
    last_codes,
    scales,
    last_scales,
    letters,
    token_forward,
    token_backward,
    halo_forward,
    halo_backward,
    short_filter,
    long_filter,
    spread,
    gather_forward,
    gather_backward,
    long_high,
    long_low,
    short_high,
    short_low,
    state,
    normed,
    masked_forward,
    masked_backward,
    keep,
    pure,
    cross,
    edge,
    taps,
    conv,
    load_sem,
    store_sem,
    piece_recv,
    cross_recv,
    mate_recv,
    halo_recv,
    z_send,
    y_send,
    x_send,
    mate_send,
    halo_send,
):
    dp, ctx = lax.axis_index("dp"), lax.axis_index("ctx")
    y, z_high = dp // 2, dp % 2
    z_low, x, core = ctx // 8, (ctx // 2) % 4, ctx % 2
    half = x % 2
    partner = dp + 1 - 2 * z_high
    ring = 4
    below, above, across = (y + 3) % ring, (y + 1) % ring, (y + 2) % ring
    up, down = ((dp + 2) % DP, ctx), ((dp + DP - 2) % DP, ctx)
    opposite = ((dp + 4) % DP, ctx)
    step = 1 - 2 * core
    beside = (dp, z_low * 8 + (x + ring + step) % ring * 2 + core)
    beside_source = (dp, z_low * 8 + (x + ring - step) % ring * 2 + core)
    mate = (dp, ctx + step)
    after, before = (dp, (ctx + 1) % CTX), (dp, (ctx + CTX - 1) % CTX)
    border = z_low // 3 + (3 - z_low) // 3
    fetches = (core + z_high) % 2

    barrier = pltpu.get_barrier_semaphore()
    for device in (up, down, opposite, beside_source, mate, after, before):
        pl.semaphore_signal(barrier, inc=1, device_id=device, device_id_type=MESH)

    @pl.when(fetches == 1)
    def _():
        shift = (z_low // 2) * 24
        source = (partner, ctx + 24 - 8 * z_low - shift)
        pl.semaphore_signal(barrier, inc=1, device_id=source, device_id_type=MESH)

    loads = []

    def load(source, target):
        index = len(loads)
        copy = pltpu.make_async_copy(source, target, load_sem.at[index])
        copy.start()
        loads.append(copy)
        return copy

    code_loads = [load(in_codes, codes), load(in_scales, scales)]
    last_loads = [load(out_codes, last_codes), load(out_scales, last_scales)]
    letter_load = load(tokens, letters)
    filter_loads = [
        load(short_source, short_filter),
        load(long_source, long_filter),
        load(long_high_source, long_high),
        load(long_low_source, long_low),
        load(short_high_source, short_high),
        load(short_low_source, short_low),
    ]
    state_loads = [
        load(hidden.at[:, pl.ds(strand * WIDTH, WIDTH)], state.at[strand]) for strand in range(2)
    ]
    table_loads = [
        load(spread_source, spread),
        load(gather_forward_source, gather_forward),
        load(gather_backward_source, gather_backward),
    ]

    def dequantise(part):
        for block in range(3):
            rows = pl.ds(pl.multiple_of(dp * SHARD + block * 32, 32), 32)
            for group in range(6):
                column = group * 128
                if part < 2:
                    place = part * 6 + group
                    values = codes[block, :, place * 128 : place * 128 + 128]
                    scale = scales[block : block + 1, place : place + 1]
                else:
                    values = last_codes[block, :, column : column + 128]
                    scale = last_scales[block : block + 1, group : group + 1]
                weights[part, rows, column : column + 128] = (values.astype(F32) * scale).astype(BF16)

    for copy in code_loads:
        copy.wait()
    dequantise(0)
    pl.semaphore_wait(barrier, 7 + 2 * border * (1 - fetches))

    def rows_of(row, side):
        return pl.ds(pl.multiple_of((2 * row + side) * SHARD, 32), SHARD)

    def piece(part, row, side):
        start = (2 * row + core) * SHARD + side * (SHARD // 2)
        return weights.at[part, pl.ds(pl.multiple_of(start, 16), SHARD // 2)]

    def remote(ref, device, sent, received):
        return pltpu.make_async_remote_copy(
            src_ref=ref,
            dst_ref=ref,
            send_sem=sent,
            recv_sem=received,
            device_id=device,
            device_id_type=MESH,
        )

    def along(part, row, device, index):
        return remote(
            piece(part, row, half), device, y_send.at[part, index], piece_recv.at[part, row]
        )

    def aside(part, row, index):
        return remote(
            piece(part, row, half), beside, x_send.at[part, index], cross_recv.at[part, row]
        )

    def to_mate(part, row, index):
        ref = weights.at[part, rows_of(row, core)]
        return remote(ref, mate, mate_send.at[part, index], mate_recv.at[part, row])

    def z_copies(part):
        sign = 1 - 2 * (z_low // 3)
        return [
            remote(
                piece(part, y, half),
                (partner, ctx + distance * sign),
                z_send.at[part, index],
                piece_recv.at[part, y],
            )
            for index, distance in enumerate((16, 24))
        ]

    def ring_copies(part):
        return [along(part, y, up, 0), along(part, y, down, 1), along(part, y, opposite, 2)]

    def owner(part, action):
        @pl.when(fetches == 0)
        def _():
            @pl.when(border == 1)
            def _():
                for copy in z_copies(part):
                    action(copy)

            for copy in ring_copies(part):
                action(copy)

    def start(copy):
        copy.start()

    def open_part(part):
        owner(part, start)

    def relay(part):
        @pl.when(fetches == 1)
        def _():
            along(part, y, up, 0).wait_recv()
            for copy in ring_copies(part):
                copy.start()
            aside(part, y, 0).start()

    def collect(part):
        for index, row in enumerate((below, above, across)):
            along(part, row, up, 0).wait_recv()
            aside(part, row, index + 1).start()

    def share(part):
        @pl.when(fetches == 1)
        def _():
            remote(
                piece(part, y, 1 - half), beside, x_send.at[part, 0], cross_recv.at[part, y]
            ).wait_recv()
            to_mate(part, y, 0).start()

        for index, row in enumerate((below, above, across)):
            remote(
                piece(part, row, 1 - half), beside, x_send.at[part, 0], cross_recv.at[part, row]
            ).wait_recv()
            to_mate(part, row, index + 1).start()

    def complete(part):
        def finish(row):
            ref = weights.at[part, rows_of(row, 1 - core)]
            remote(ref, mate, mate_send.at[part, 0], mate_recv.at[part, row]).wait_recv()

        @pl.when(fetches == 0)
        def _():
            finish(y)

        for row in (below, above, across):
            finish(row)

    halos = []

    def halo(source, target, device):
        index = len(halos)
        copy = pltpu.make_async_remote_copy(
            src_ref=source,
            dst_ref=target,
            send_sem=halo_send.at[index],
            recv_sem=halo_recv.at[index],
            device_id=device,
            device_id_type=MESH,
        )
        copy.start()
        halos.append(copy)

    open_part(0)
    for copy in last_loads:
        copy.wait()
    dequantise(1)
    open_part(1)
    dequantise(2)
    open_part(2)
    letter_load.wait()
    halo(letters.at[:, pl.ds(ROWS - 256, 256)], token_forward, after)
    halo(letters.at[:, pl.ds(0, 256)], token_backward, before)
    halo(hidden.at[pl.ds(ROWS - HALO, HALO), pl.ds(0, WIDTH)], halo_forward, after)
    halo(hidden.at[pl.ds(0, HALO), pl.ds(WIDTH, WIDTH)], halo_backward, before)

    def keep_rows(values, live):
        flags = jnp.where(values != 4, live, 0.0)
        return jnp.transpose(jnp.broadcast_to(flags, (128, 128)))

    one = jnp.float32(1.0)
    for block in range(ROWS // 128):
        keep[block * 128 + 256 : block * 128 + 384] = keep_rows(
            letters[:, block * 128 : block * 128 + 128], one
        )

    def project(values):
        wide = values.astype(F32)
        mean = jnp.mean(wide * wide, axis=-1, keepdims=True)
        return (wide * lax.rsqrt(mean + 1e-5)).astype(BF16)

    for copy in state_loads:
        copy.wait()

    def norm_pass(part, carry):
        rows = pl.ds(pl.multiple_of(part * PART, PART), PART)
        for strand in range(2):
            start = part // 2 * (2 * TILE) + strand * TILE + part % 2 * PART
            normed[pl.ds(pl.multiple_of(start, PART), PART)] = project(state[strand, rows])
        return carry

    lax.fori_loop(0, 1, norm_pass, 0)
    relay(0)
    lax.fori_loop(1, 3, norm_pass, 0)
    relay(1)
    lax.fori_loop(3, 4, norm_pass, 0)
    relay(2)
    collect(0)
    collect(1)

    for copy in filter_loads:
        copy.wait()
    short = short_filter[...].astype(F32)
    long = long_filter[...]
    padded = jnp.concatenate([short, jnp.zeros((16 - SHORT, WIDTH), F32)], axis=0).astype(BF16)
    dot = functools.partial(jnp.dot, preferred_element_type=F32)
    long_hat = dot(long_high[...], long) + dot(long_low[...], long)
    short_hat = dot(short_high[...], padded) + dot(short_low[...], padded)
    real_long, imag_long = long_hat[:BLOCK], long_hat[BLOCK:]
    real_short, imag_short = short_hat[:BLOCK], short_hat[BLOCK:]
    first = lax.broadcasted_iota(jnp.int32, (BLOCK, WIDTH), 0) == 0
    scale = jnp.where(first, 1.0 / SPAN, 2.0 / SPAN)
    reals, imags = real_short * real_long, imag_short * imag_long
    pure[...] = jnp.where(first, reals, reals - imags) * scale
    edge[...] = jnp.where(first, imags, reals - imags) * scale
    cross[...] = jnp.where(first, 0.0, real_short * imag_long + imag_short * real_long) * scale
    long_head = long[:16].astype(F32)
    taps[0:1] = short[0:1] * long_head[0:1]
    taps[1:2] = short[0:1] * long_head[1:2] + short[1:2] * long_head[0:1]

    for copy in table_loads:
        copy.wait()
    share(0)
    collect(2)
    complete(0)

    def value_part(norm, flags):
        return (dot(norm, weights[0]) * jnp.tile(flags, (1, 6))).astype(BF16)

    def value_pass(tile, carry):
        start = pl.multiple_of(tile * TILE, TILE)
        values = dot(normed[pl.ds(pl.multiple_of(tile * 2 * TILE, TILE), 2 * TILE)], weights[0])
        flags = jnp.tile(keep[pl.ds(start + 256, TILE)], (1, 6))
        masked_forward[pl.ds(pl.multiple_of(start + HALO, 16), TILE)] = (
            values[:TILE] * flags
        ).astype(BF16)
        masked_backward[pl.ds(start, TILE)] = (values[TILE:] * flags).astype(BF16)
        return carry

    lax.fori_loop(0, 1, value_pass, 0)
    share(1)
    share(2)
    lax.fori_loop(1, ROWS // TILE, value_pass, 0)

    for copy in halos:
        copy.wait_recv()
    live_before = jnp.where(ctx > 0, 1.0, 0.0)
    live_after = jnp.where(ctx < CTX - 1, 1.0, 0.0)
    for block in range(2):
        columns = slice(block * 128, block * 128 + 128)
        keep[columns] = keep_rows(token_forward[:, columns], live_before)
        keep[ROWS + 256 + block * 128 : ROWS + 384 + block * 128] = keep_rows(
            token_backward[:, columns], live_after
        )
    masked_forward[0:HALO] = value_part(project(halo_forward[...]), keep[256 - HALO : 256])
    masked_backward[ROWS : ROWS + HALO] = value_part(
        project(halo_backward[...]), keep[ROWS + 256 : ROWS + 256 + HALO]
    )
    complete(1)

    def filtered(strand, start, target):
        masked = masked_backward if strand else masked_forward
        origin = start if strand else pl.multiple_of(start + 16, 16)
        window = masked[pl.ds(origin, SPAN)]
        waves = dot(spread[...], window)
        real, imag = waves[:BLOCK], waves[BLOCK:]
        straight, turned = real * pure[...], imag * cross[...]
        upright, bent = imag * edge[...], real * cross[...]
        if strand:
            parts = [straight + turned, upright - bent]
        else:
            parts = [straight - turned, upright + bent]
        product = jnp.concatenate([part.astype(BF16) for part in parts], axis=0)
        gather = gather_backward if strand else gather_forward
        conv[target : target + BLOCK] = dot(gather[...], product)
        last, second = taps[0:1], taps[1:2]
        row = lax.broadcasted_iota(jnp.int32, (8, WIDTH), 0)
        if strand:
            wrong = masked[pl.ds(start, 16)].astype(F32)
            right = masked[pl.ds(pl.multiple_of(start + SPAN, 16), 16)].astype(F32)
            gap = right - wrong
            outer, inner = gap[0:1], gap[1:2]
            fix = jnp.where(row == 7, second * outer + last * inner, 0.0)
            fix = fix + jnp.where(row == 6, last * outer, 0.0)
            conv[target + BLOCK - 8 : target + BLOCK] += fix
        else:
            right = masked[pl.ds(start, 16)].astype(F32)
            wrong = masked[pl.ds(pl.multiple_of(start + SPAN, 16), 16)].astype(F32)
            gap = right - wrong
            outer, inner = gap[15:16], gap[14:15]
            fix = jnp.where(row == 0, second * outer + last * inner, 0.0)
            fix = fix + jnp.where(row == 1, last * outer, 0.0)
            conv[target : target + 8] += fix

    def store(tile):
        rows = pl.ds(pl.multiple_of(tile * 2 * TILE, TILE), 2 * TILE)
        return pltpu.make_async_copy(normed.at[rows], gated_out.at[rows], store_sem.at[tile])

    def gate_pass(tile, carry):
        start = pl.multiple_of(tile * TILE, TILE)
        rows = pl.ds(pl.multiple_of(tile * 2 * TILE, TILE), 2 * TILE)
        for strand in range(2):
            for block in range(TILE // BLOCK):
                filtered(
                    strand,
                    pl.multiple_of(start + block * BLOCK, BLOCK),
                    strand * TILE + block * BLOCK,
                )
        half_gate = 0.5 * dot(normed[rows], weights[1])
        gated = (half_gate * jnp.tanh(half_gate) + half_gate) * conv[...]
        normed[rows] = gated.astype(BF16)
        store(tile).start()
        return carry

    lax.fori_loop(0, ROWS // TILE - 1, gate_pass, 0)
    complete(2)
    last_store = pltpu.make_async_copy(weights.at[2], last_weights, store_sem.at[ROWS // TILE])
    last_store.start()
    lax.fori_loop(ROWS // TILE - 1, ROWS // TILE, gate_pass, 0)

    for copy in halos:
        copy.wait_send()
    for part in range(3):
        owner(part, lambda copy: copy.wait_send())

        @pl.when(fetches == 1)
        def _(part=part):
            for copy in ring_copies(part):
                copy.wait_send()
            aside(part, y, 0).wait_send()
            to_mate(part, y, 0).wait_send()

        for index, row in enumerate((below, above, across)):
            aside(part, row, index + 1).wait_send()
            to_mate(part, row, index + 1).wait_send()
    for tile in range(ROWS // TILE):
        store(tile).wait()
    last_store.wait()


def finish_kernel(
    hidden, gated_source, weight_source, out, weight, gated, state, load_sem, ready_sem, store_sem
):
    def fetch(unit):
        rows = pl.ds(pl.multiple_of(unit // 2 * TILE, TILE), TILE)
        columns = pl.ds(pl.multiple_of(unit % 2 * WIDTH, 128), WIDTH)
        own = pl.ds(pl.multiple_of(unit * TILE, TILE), TILE)
        return (
            pltpu.make_async_copy(gated_source.at[own], gated.at[own], load_sem.at[unit]),
            pltpu.make_async_copy(hidden.at[rows, columns], state.at[own], ready_sem.at[unit]),
            pltpu.make_async_copy(state.at[own], out.at[rows, columns], store_sem.at[unit]),
        )

    units = 2 * ROWS // TILE
    first = pltpu.make_async_copy(weight_source, weight, load_sem.at[units])
    first.start()
    for unit in range(units):
        for copy in fetch(unit)[:2]:
            copy.start()
    first.wait()

    def out_pass(unit, carry):
        own = pl.ds(pl.multiple_of(unit * TILE, TILE), TILE)
        *loads, store = fetch(unit)
        for copy in loads:
            copy.wait()
        branch = jnp.dot(gated[own], weight[...], preferred_element_type=F32)
        state[own] = (state[own].astype(F32) + branch).astype(BF16)
        store.start()
        return carry

    lax.fori_loop(0, units, out_pass, 0)
    for unit in range(units):
        fetch(unit)[2].wait()


def shards(
    hidden_state, tokens, in_codes, in_scales, out_codes, out_scales, short_filter, long_filter
):
    window = hidden_state[0]
    anywhere = pl.BlockSpec(memory_space=pl.ANY)
    dma = pltpu.SemaphoreType.DMA
    tables = constants()
    gated, last_weights = pl.pallas_call(
        layer_kernel,
        out_shape=(
            jax.ShapeDtypeStruct((2 * ROWS, WIDTH), BF16),
            jax.ShapeDtypeStruct((WIDTH, WIDTH), BF16),
        ),
        in_specs=[anywhere] * (8 + len(tables)),
        out_specs=(anywhere, anywhere),
        scratch_shapes=[
            pltpu.VMEM((3, WIDTH, WIDTH), BF16),
            pltpu.VMEM((3, 32, 2 * WIDTH), BF16),
            pltpu.VMEM((3, 32, WIDTH), BF16),
            pltpu.VMEM((3, 12), F32),
            pltpu.VMEM((3, 6), F32),
            pltpu.VMEM((1, ROWS), jnp.int32),
            pltpu.VMEM((1, 256), jnp.int32),
            pltpu.VMEM((1, 256), jnp.int32),
            pltpu.VMEM((HALO, WIDTH), BF16),
            pltpu.VMEM((HALO, WIDTH), BF16),
            pltpu.VMEM((SHORT, WIDTH), BF16),
            pltpu.VMEM((LONG, WIDTH), BF16),
            *(pltpu.VMEM(table.shape, BF16) for table in tables),
            pltpu.VMEM((2, ROWS, WIDTH), BF16),
            pltpu.VMEM((2 * ROWS, WIDTH), BF16),
            pltpu.VMEM((ROWS + HALO, WIDTH), BF16),
            pltpu.VMEM((ROWS + HALO, WIDTH), BF16),
            pltpu.VMEM((ROWS + 512, 128), F32),
            pltpu.VMEM((BLOCK, WIDTH), F32),
            pltpu.VMEM((BLOCK, WIDTH), F32),
            pltpu.VMEM((BLOCK, WIDTH), F32),
            pltpu.VMEM((8, WIDTH), F32),
            pltpu.VMEM((2 * TILE, WIDTH), F32),
            dma((16,)),
            dma((4,)),
            dma((3, 4)),
            dma((3, 4)),
            dma((3, 4)),
            dma((4,)),
            dma((3, 2)),
            dma((3, 3)),
            dma((3, 4)),
            dma((3, 4)),
            dma((4,)),
        ],
        compiler_params=pltpu.CompilerParams(
            collective_id=0, has_side_effects=True, vmem_limit_bytes=VMEM_LIMIT
        ),
        name="layer",
    )(
        window,
        tokens,
        in_codes,
        in_scales,
        out_codes,
        out_scales,
        short_filter,
        long_filter,
        *map(jnp.asarray, tables),
    )
    result = pl.pallas_call(
        finish_kernel,
        out_shape=jax.ShapeDtypeStruct((ROWS, 2 * WIDTH), BF16),
        in_specs=[anywhere] * 3,
        out_specs=anywhere,
        scratch_shapes=[
            pltpu.VMEM((WIDTH, WIDTH), BF16),
            pltpu.VMEM((2 * ROWS, WIDTH), BF16),
            pltpu.VMEM((2 * ROWS, WIDTH), BF16),
            dma((8,)),
            dma((8,)),
            dma((8,)),
        ],
        compiler_params=pltpu.CompilerParams(vmem_limit_bytes=VMEM_LIMIT),
        name="finish",
    )(window, gated, last_weights)
    return result[None]


def solution(mesh):
    in_specs = (
        P("dp", "ctx", None),
        P("dp", "ctx"),
        P("dp", None, None),
        P("dp", None),
        P("dp", None, None),
        P("dp", None),
        P(),
        P(),
    )
    out_specs = P("dp", "ctx", None)
    return jax.shard_map(shards, mesh=mesh, in_specs=in_specs, out_specs=out_specs, check_vma=False)
```

```python
import functools

import jax
import jax.numpy as jnp
import numpy as np
from jax import lax
from jax.experimental import pallas as pl
from jax.experimental.pallas import tpu as pltpu
from jax.sharding import PartitionSpec as P

MESH = pl.DeviceIdType.MESH
F32, BF16 = jnp.float32, jnp.bfloat16
ROWS, HALO = 1024, 144
WIDTH, SHARD, OWN = 768, 96, 384
BLOCK, SPAN = 128, 256
TILE = 256
DP, CTX = 8, 32
LONG, SHORT = 128, 4
VMEM_LIMIT = 63 << 20


def transform(positions):
    freq = np.arange(BLOCK)[:, None]
    angle = 2 * np.pi * ((freq * positions[None, :]) % SPAN) / SPAN
    real, imag = np.cos(angle), -np.sin(angle)
    imag[0] = np.cos(np.pi * (positions % 2))
    return np.concatenate([real, imag], axis=0)


def split(matrix):
    high = matrix.astype(np.float32).astype(BF16)
    return high, (matrix - high.astype(np.float64)).astype(np.float32).astype(BF16)


def constants():
    spread = transform(np.arange(SPAN))
    long_high, long_low = split(transform(LONG - 1 - np.arange(LONG)))
    short_table = np.zeros((SPAN, 16))
    short_table[:, :SHORT] = transform(SHORT - 1 - np.arange(SHORT))
    short_high, short_low = split(short_table)
    as_bf16 = lambda table: table.astype(np.float32).astype(BF16)
    gather_forward = as_bf16(spread[:, BLOCK:].T)
    gather_backward = as_bf16(spread[:, :BLOCK].T)
    return (
        as_bf16(spread),
        gather_forward,
        gather_backward,
        long_high,
        long_low,
        short_high,
        short_low,
    )


def layer_kernel(
    hidden,
    tokens,
    in_codes,
    in_scales,
    out_codes,
    out_scales,
    short_source,
    long_source,
    spread_source,
    gather_forward_source,
    gather_backward_source,
    long_high_source,
    long_low_source,
    short_high_source,
    short_low_source,
    gated_out,
    last_weights,
    weights,
    codes,
    last_codes,
    scales,
    last_scales,
    letters,
    token_forward,
    token_backward,
    halo_forward,
    halo_backward,
    short_filter,
    long_filter,
    spread,
    gather_forward,
    gather_backward,
    long_high,
    long_low,
    short_high,
    short_low,
    state,
    normed,
    masked_forward,
    masked_backward,
    keep,
    pure,
    cross,
    edge,
    taps,
    conv,
    values_sum,
    gate_sum,
    load_sem,
    store_sem,
    piece_recv,
    cross_recv,
    mate_recv,
    halo_recv,
    z_send,
    y_send,
    x_send,
    mate_send,
    halo_send,
):
    dp, ctx = lax.axis_index("dp"), lax.axis_index("ctx")
    y, z_high = dp // 2, dp % 2
    z_low, x, core = ctx // 8, (ctx // 2) % 4, ctx % 2
    half = x % 2
    partner = dp + 1 - 2 * z_high
    ring = 4
    below, above, across = (y + 3) % ring, (y + 1) % ring, (y + 2) % ring
    up, down = ((dp + 2) % DP, ctx), ((dp + DP - 2) % DP, ctx)
    opposite = ((dp + 4) % DP, ctx)
    step = 1 - 2 * core

    def along_x(distance):
        return (dp, z_low * 8 + (x + ring + distance) % ring * 2 + core)

    beside = along_x(step)
    mate = (dp, ctx + step)
    after, before = (dp, (ctx + 1) % CTX), (dp, (ctx + CTX - 1) % CTX)
    border = z_low // 3 + (3 - z_low) // 3
    fetches = (core + z_high) % 2

    barrier = pltpu.get_barrier_semaphore()
    for device in (up, down, opposite, along_x(-step), mate, after, before):
        pl.semaphore_signal(barrier, inc=1, device_id=device, device_id_type=MESH)

    @pl.when(fetches == 1)
    def _():
        shift = (z_low // 2) * 24
        source = (partner, ctx + 24 - 8 * z_low - shift)
        pl.semaphore_signal(barrier, inc=1, device_id=source, device_id_type=MESH)

    loads = []

    def load(source, target):
        index = len(loads)
        copy = pltpu.make_async_copy(source, target, load_sem.at[index])
        copy.start()
        loads.append(copy)
        return copy

    code_loads = [load(in_codes, codes), load(in_scales, scales)]
    last_loads = [load(out_codes, last_codes), load(out_scales, last_scales)]
    letter_load = load(tokens, letters)
    filter_loads = [
        load(short_source, short_filter),
        load(long_source, long_filter),
        load(long_high_source, long_high),
        load(long_low_source, long_low),
        load(short_high_source, short_high),
        load(short_low_source, short_low),
    ]
    state_loads = [
        load(hidden.at[:, pl.ds(strand * WIDTH, WIDTH)], state.at[strand]) for strand in range(2)
    ]
    table_loads = [
        load(spread_source, spread),
        load(gather_forward_source, gather_forward),
        load(gather_backward_source, gather_backward),
    ]

    def base_of(part, row, side):
        if part == 2:
            return (2 * row + side) * SHARD
        return (side + z_high) % 2 * OWN + row * SHARD

    def dequantise(part):
        for block in range(3):
            start = base_of(part, y, z_high) + block * 32
            rows = pl.ds(pl.multiple_of(start, 32), 32)
            for group in range(6):
                column = group * 128
                if part < 2:
                    place = part * 6 + group
                    values = codes[block, :, place * 128 : place * 128 + 128]
                    scale = scales[block : block + 1, place : place + 1]
                else:
                    values = last_codes[block, :, column : column + 128]
                    scale = last_scales[block : block + 1, group : group + 1]
                weights[part, rows, column : column + 128] = (values.astype(F32) * scale).astype(BF16)

    for copy in code_loads:
        copy.wait()
    dequantise(0)
    pl.semaphore_wait(barrier, 7 + 2 * border * (1 - fetches))

    def piece(part, row, side, base=None):
        start = (base_of(part, row, core) if base is None else base) + side * (SHARD // 2)
        return weights.at[part, pl.ds(pl.multiple_of(start, 16), SHARD // 2)]

    def remote(ref, device, sent, received, target=None):
        return pltpu.make_async_remote_copy(
            src_ref=ref,
            dst_ref=ref if target is None else target,
            send_sem=sent,
            recv_sem=received,
            device_id=device,
            device_id_type=MESH,
        )

    def along(part, row, device, index):
        return remote(
            piece(part, row, half), device, y_send.at[part, index], piece_recv.at[part, row]
        )

    def aside(part, row, index):
        return remote(
            piece(part, row, half),
            beside,
            x_send.at[part, index],
            cross_recv.at[part, row],
        )

    def to_mate(part, row, side, index):
        return remote(
            piece(part, row, side), mate, mate_send.at[part, index], mate_recv.at[part, row]
        )

    def z_copies(part):
        sign = 1 - 2 * (z_low // 3)
        return [
            remote(
                piece(part, y, half),
                (partner, ctx + distance * sign),
                z_send.at[part, index],
                piece_recv.at[part, y],
                piece(part, y, half, None if part == 2 else OWN + y * SHARD),
            )
            for index, distance in enumerate((16, 24))
        ]

    def ring_copies(part):
        return [along(part, y, up, 0), along(part, y, down, 1), along(part, y, opposite, 2)]

    def owner(part, action):
        @pl.when(fetches == 0)
        def _():
            @pl.when(border == 1)
            def _():
                for copy in z_copies(part):
                    action(copy)

            for copy in ring_copies(part):
                action(copy)

    def start(copy):
        copy.start()

    def open_part(part):
        owner(part, start)

    def relay(part):
        @pl.when(fetches == 1)
        def _():
            along(part, y, up, 0).wait_recv()
            for copy in ring_copies(part):
                copy.start()
            aside(part, y, 0).start()
            to_mate(part, y, half, 0).start()

    def collect(part):
        for index, row in enumerate((below, above, across)):
            along(part, row, up, 0).wait_recv()
            aside(part, row, index + 1).start()
            to_mate(part, row, half, 2 * index + 2).start()

    def share(part):
        def pass_on(row, index):
            remote(
                piece(part, row, 1 - half), beside, x_send.at[part, 0], cross_recv.at[part, row]
            ).wait_recv()
            to_mate(part, row, 1 - half, index).start()

        @pl.when(fetches == 1)
        def _():
            pass_on(y, 1)

        for index, row in enumerate((below, above, across)):
            pass_on(row, 2 * index + 3)

    def complete(part, role):
        def finish(row):
            start = base_of(part, row, 1 - core)
            ref = weights.at[part, pl.ds(pl.multiple_of(start, 32), SHARD)]
            remote(ref, mate, mate_send.at[part, 0], mate_recv.at[part, row]).wait_recv()

        @pl.when(fetches == role)
        def _():
            if role == 0:
                finish(y)
            for row in (below, above, across):
                finish(row)

    halos = []

    def halo(source, target, device):
        index = len(halos)
        copy = pltpu.make_async_remote_copy(
            src_ref=source,
            dst_ref=target,
            send_sem=halo_send.at[index],
            recv_sem=halo_recv.at[index],
            device_id=device,
            device_id_type=MESH,
        )
        copy.start()
        halos.append(copy)

    open_part(0)
    for copy in last_loads:
        copy.wait()
    dequantise(1)
    open_part(1)
    dequantise(2)
    open_part(2)
    letter_load.wait()
    halo(letters.at[:, pl.ds(ROWS - 256, 256)], token_forward, after)
    halo(letters.at[:, pl.ds(0, 256)], token_backward, before)
    halo(hidden.at[pl.ds(ROWS - HALO, HALO), pl.ds(0, WIDTH)], halo_forward, after)
    halo(hidden.at[pl.ds(0, HALO), pl.ds(WIDTH, WIDTH)], halo_backward, before)

    def keep_rows(values, live):
        flags = jnp.where(values != 4, live, 0.0)
        return jnp.transpose(jnp.broadcast_to(flags, (128, 128)))

    one = jnp.float32(1.0)
    for block in range(ROWS // 128):
        keep[block * 128 + 256 : block * 128 + 384] = keep_rows(
            letters[:, block * 128 : block * 128 + 128], one
        )

    def project(values):
        wide = values.astype(F32)
        mean = jnp.mean(wide * wide, axis=-1, keepdims=True)
        scaled = wide * lax.rsqrt(mean + 1e-5)
        low, high = (
            jnp.concatenate(
                [scaled[:, start : start + SHARD] for start in range(side * SHARD, WIDTH, 2 * SHARD)],
                axis=1,
            )
            for side in range(2)
        )
        own_first = z_high == 0
        ordered = [jnp.where(own_first, low, high), jnp.where(own_first, high, low)]
        return jnp.concatenate([item.astype(BF16) for item in ordered], axis=1)

    for copy in state_loads:
        copy.wait()

    def norm_pass(tile, carry):
        rows = pl.ds(pl.multiple_of(tile * TILE, TILE), TILE)
        for strand in range(2):
            start = (2 * tile + strand) * TILE
            normed[pl.ds(pl.multiple_of(start, TILE), TILE)] = project(state[strand, rows])
        return carry

    lax.fori_loop(0, 1, norm_pass, 0)
    relay(0)
    lax.fori_loop(1, 3, norm_pass, 0)
    relay(1)
    lax.fori_loop(3, 4, norm_pass, 0)
    relay(2)
    collect(0)
    collect(1)

    for copy in filter_loads:
        copy.wait()
    short = short_filter[...].astype(F32)
    long = long_filter[...]
    padded = jnp.concatenate([short, jnp.zeros((16 - SHORT, WIDTH), F32)], axis=0).astype(BF16)
    dot = functools.partial(jnp.dot, preferred_element_type=F32)
    long_hat = dot(long_high[...], long) + dot(long_low[...], long)
    short_hat = dot(short_high[...], padded) + dot(short_low[...], padded)
    real_long, imag_long = long_hat[:BLOCK], long_hat[BLOCK:]
    real_short, imag_short = short_hat[:BLOCK], short_hat[BLOCK:]
    first = lax.broadcasted_iota(jnp.int32, (BLOCK, WIDTH), 0) == 0
    scale = jnp.where(first, 1.0 / SPAN, 2.0 / SPAN)
    reals, imags = real_short * real_long, imag_short * imag_long
    pure[...] = jnp.where(first, reals, reals - imags) * scale
    edge[...] = jnp.where(first, imags, reals - imags) * scale
    cross[...] = jnp.where(first, 0.0, real_short * imag_long + imag_short * real_long) * scale
    long_head = long[:16].astype(F32)
    taps[0:1] = short[0:1] * long_head[0:1]
    taps[1:2] = short[0:1] * long_head[1:2] + short[1:2] * long_head[0:1]

    for copy in table_loads:
        copy.wait()
    share(0)
    collect(2)
    share(1)
    complete(0, 1)
    complete(1, 1)

    def rows_in(tile):
        return pl.ds(pl.multiple_of(tile * 2 * TILE, TILE), 2 * TILE)

    def own_pass(tile, carry):
        rows = rows_in(tile)
        values_sum[rows] = dot(normed[rows, :OWN], weights[0, :OWN])
        gate_sum[rows] = dot(normed[rows, :OWN], weights[1, :OWN])
        return carry

    lax.fori_loop(0, ROWS // TILE, own_pass, 0)
    share(2)
    complete(0, 0)

    def value_part(norm, flags):
        return (dot(norm, weights[0]) * jnp.tile(flags, (1, 6))).astype(BF16)

    def value_pass(tile, carry):
        start = pl.multiple_of(tile * TILE, TILE)
        rows = rows_in(tile)
        values = values_sum[rows] + dot(normed[rows, OWN:], weights[0, OWN:])
        flags = jnp.tile(keep[pl.ds(start + 256, TILE)], (1, 6))
        masked_forward[pl.ds(pl.multiple_of(start + HALO, 16), TILE)] = (
            values[:TILE] * flags
        ).astype(BF16)
        masked_backward[pl.ds(start, TILE)] = (values[TILE:] * flags).astype(BF16)
        return carry

    lax.fori_loop(0, ROWS // TILE, value_pass, 0)

    for copy in halos:
        copy.wait_recv()
    live_before = jnp.where(ctx > 0, 1.0, 0.0)
    live_after = jnp.where(ctx < CTX - 1, 1.0, 0.0)
    for block in range(2):
        columns = slice(block * 128, block * 128 + 128)
        keep[columns] = keep_rows(token_forward[:, columns], live_before)
        keep[ROWS + 256 + block * 128 : ROWS + 384 + block * 128] = keep_rows(
            token_backward[:, columns], live_after
        )
    masked_forward[0:HALO] = value_part(project(halo_forward[...]), keep[256 - HALO : 256])
    masked_backward[ROWS : ROWS + HALO] = value_part(
        project(halo_backward[...]), keep[ROWS + 256 : ROWS + 256 + HALO]
    )
    complete(1, 0)

    def filtered(strand, start, target):
        masked = masked_backward if strand else masked_forward
        origin = start if strand else pl.multiple_of(start + 16, 16)
        window = masked[pl.ds(origin, SPAN)]
        waves = dot(spread[...], window)
        real, imag = waves[:BLOCK], waves[BLOCK:]
        straight, turned = real * pure[...], imag * cross[...]
        upright, bent = imag * edge[...], real * cross[...]
        if strand:
            parts = [straight + turned, upright - bent]
        else:
            parts = [straight - turned, upright + bent]
        product = jnp.concatenate([part.astype(BF16) for part in parts], axis=0)
        gather = gather_backward if strand else gather_forward
        conv[target : target + BLOCK] = dot(gather[...], product)
        last, second = taps[0:1], taps[1:2]
        row = lax.broadcasted_iota(jnp.int32, (8, WIDTH), 0)
        if strand:
            wrong = masked[pl.ds(start, 16)].astype(F32)
            right = masked[pl.ds(pl.multiple_of(start + SPAN, 16), 16)].astype(F32)
            gap = right - wrong
            outer, inner = gap[0:1], gap[1:2]
            fix = jnp.where(row == 7, second * outer + last * inner, 0.0)
            fix = fix + jnp.where(row == 6, last * outer, 0.0)
            conv[target + BLOCK - 8 : target + BLOCK] += fix
        else:
            right = masked[pl.ds(start, 16)].astype(F32)
            wrong = masked[pl.ds(pl.multiple_of(start + SPAN, 16), 16)].astype(F32)
            gap = right - wrong
            outer, inner = gap[15:16], gap[14:15]
            fix = jnp.where(row == 0, second * outer + last * inner, 0.0)
            fix = fix + jnp.where(row == 1, last * outer, 0.0)
            conv[target : target + 8] += fix

    def store(tile):
        rows = rows_in(tile)
        return pltpu.make_async_copy(normed.at[rows], gated_out.at[rows], store_sem.at[tile])

    def gate_pass(tile, carry):
        start = pl.multiple_of(tile * TILE, TILE)
        rows = rows_in(tile)
        for strand in range(2):
            for block in range(TILE // BLOCK):
                offset = block * BLOCK
                filtered(strand, pl.multiple_of(start + offset, BLOCK), strand * TILE + offset)
        gate = gate_sum[rows] + dot(normed[rows, OWN:], weights[1, OWN:])
        half_gate = 0.5 * gate
        gated = (half_gate * jnp.tanh(half_gate) + half_gate) * conv[...]
        normed[rows] = gated.astype(BF16)
        store(tile).start()
        return carry

    lax.fori_loop(0, 3, gate_pass, 0)
    complete(2, 0)
    complete(2, 1)
    last_store = pltpu.make_async_copy(weights.at[2], last_weights, store_sem.at[ROWS // TILE])
    last_store.start()
    lax.fori_loop(ROWS // TILE - 1, ROWS // TILE, gate_pass, 0)

    for copy in halos:
        copy.wait_send()
    for part in range(3):
        owner(part, lambda copy: copy.wait_send())

        @pl.when(fetches == 1)
        def _(part=part):
            for copy in ring_copies(part):
                copy.wait_send()
            aside(part, y, 0).wait_send()
            for side in range(2):
                to_mate(part, y, side, side).wait_send()

        for index, row in enumerate((below, above, across)):
            aside(part, row, index + 1).wait_send()
            for side in range(2):
                to_mate(part, row, side, 2 * index + 2 + side).wait_send()
    for tile in range(ROWS // TILE):
        store(tile).wait()
    last_store.wait()


def finish_kernel(
    hidden, gated_source, weight_source, out, weight, gated, state, load_sem, ready_sem, store_sem
):
    def fetch(unit):
        rows = pl.ds(pl.multiple_of(unit * TILE, TILE), TILE)
        own = pl.ds(pl.multiple_of(unit * 2 * TILE, TILE), 2 * TILE)
        return (
            pltpu.make_async_copy(gated_source.at[own], gated.at[own], load_sem.at[unit]),
            pltpu.make_async_copy(hidden.at[rows], state.at[rows], ready_sem.at[unit]),
            pltpu.make_async_copy(state.at[rows], out.at[rows], store_sem.at[unit]),
        )

    units = ROWS // TILE
    first = pltpu.make_async_copy(weight_source, weight, load_sem.at[units])
    first.start()
    for unit in range(units):
        for copy in fetch(unit)[:2]:
            copy.start()
    first.wait()

    def out_pass(unit, carry):
        rows = pl.ds(pl.multiple_of(unit * TILE, TILE), TILE)
        own = pl.ds(pl.multiple_of(unit * 2 * TILE, TILE), 2 * TILE)
        *loads, store = fetch(unit)
        for copy in loads:
            copy.wait()
        branch = jnp.dot(gated[own], weight[...], preferred_element_type=F32)
        for strand in range(2):
            columns = slice(strand * WIDTH, strand * WIDTH + WIDTH)
            added = branch[strand * TILE : strand * TILE + TILE]
            state[rows, columns] = (state[rows, columns].astype(F32) + added).astype(BF16)
        store.start()
        return carry

    lax.fori_loop(0, units, out_pass, 0)
    for unit in range(units):
        fetch(unit)[2].wait()


def shards(
    hidden_state, tokens, in_codes, in_scales, out_codes, out_scales, short_filter, long_filter
):
    window = hidden_state[0]
    anywhere = pl.BlockSpec(memory_space=pl.ANY)
    dma = pltpu.SemaphoreType.DMA
    tables = constants()
    gated, last_weights = pl.pallas_call(
        layer_kernel,
        out_shape=(
            jax.ShapeDtypeStruct((2 * ROWS, WIDTH), BF16),
            jax.ShapeDtypeStruct((WIDTH, WIDTH), BF16),
        ),
        in_specs=[anywhere] * (8 + len(tables)),
        out_specs=(anywhere, anywhere),
        scratch_shapes=[
            pltpu.VMEM((3, WIDTH, WIDTH), BF16),
            pltpu.VMEM((3, 32, 2 * WIDTH), BF16),
            pltpu.VMEM((3, 32, WIDTH), BF16),
            pltpu.VMEM((3, 12), F32),
            pltpu.VMEM((3, 6), F32),
            pltpu.VMEM((1, ROWS), jnp.int32),
            pltpu.VMEM((1, 256), jnp.int32),
            pltpu.VMEM((1, 256), jnp.int32),
            pltpu.VMEM((HALO, WIDTH), BF16),
            pltpu.VMEM((HALO, WIDTH), BF16),
            pltpu.VMEM((SHORT, WIDTH), BF16),
            pltpu.VMEM((LONG, WIDTH), BF16),
            *(pltpu.VMEM(table.shape, BF16) for table in tables),
            pltpu.VMEM((2, ROWS, WIDTH), BF16),
            pltpu.VMEM((2 * ROWS, WIDTH), BF16),
            pltpu.VMEM((ROWS + HALO, WIDTH), BF16),
            pltpu.VMEM((ROWS + HALO, WIDTH), BF16),
            pltpu.VMEM((ROWS + 512, 128), F32),
            pltpu.VMEM((BLOCK, WIDTH), F32),
            pltpu.VMEM((BLOCK, WIDTH), F32),
            pltpu.VMEM((BLOCK, WIDTH), F32),
            pltpu.VMEM((8, WIDTH), F32),
            pltpu.VMEM((2 * TILE, WIDTH), F32),
            pltpu.VMEM((2 * ROWS, WIDTH), F32),
            pltpu.VMEM((2 * ROWS, WIDTH), F32),
            dma((16,)),
            dma((8,)),
            dma((3, 4)),
            dma((3, 4)),
            dma((3, 4)),
            dma((4,)),
            dma((3, 2)),
            dma((3, 3)),
            dma((3, 4)),
            dma((3, 8)),
            dma((4,)),
        ],
        compiler_params=pltpu.CompilerParams(
            collective_id=0, has_side_effects=True, vmem_limit_bytes=VMEM_LIMIT
        ),
        name="layer",
    )(
        window,
        tokens,
        in_codes,
        in_scales,
        out_codes,
        out_scales,
        short_filter,
        long_filter,
        *map(jnp.asarray, tables),
    )
    result = pl.pallas_call(
        finish_kernel,
        out_shape=jax.ShapeDtypeStruct((ROWS, 2 * WIDTH), BF16),
        in_specs=[anywhere] * 3,
        out_specs=anywhere,
        scratch_shapes=[
            pltpu.VMEM((WIDTH, WIDTH), BF16),
            pltpu.VMEM((2 * ROWS, WIDTH), BF16),
            pltpu.VMEM((ROWS, 2 * WIDTH), BF16),
            dma((8,)),
            dma((8,)),
            dma((8,)),
        ],
        compiler_params=pltpu.CompilerParams(vmem_limit_bytes=VMEM_LIMIT),
        name="finish",
    )(window, gated, last_weights)
    return result[None]


def solution(mesh):
    in_specs = (
        P("dp", "ctx", None),
        P("dp", "ctx"),
        P("dp", None, None),
        P("dp", None),
        P("dp", None, None),
        P("dp", None),
        P(),
        P(),
    )
    out_specs = P("dp", "ctx", None)
    return jax.shard_map(shards, mesh=mesh, in_specs=in_specs, out_specs=out_specs, check_vma=False)
```

```python
import functools

import jax
import jax.numpy as jnp
import numpy as np
from jax import lax
from jax.experimental import pallas as pl
from jax.experimental.pallas import tpu as pltpu
from jax.sharding import PartitionSpec as P

MESH = pl.DeviceIdType.MESH
F32, BF16 = jnp.float32, jnp.bfloat16
ROWS, HALO = 1024, 144
WIDTH, SHARD = 768, 96
BLOCK, SPAN = 128, 256
TILE = 256
DP, CTX = 8, 32
LONG, SHORT = 128, 4
VMEM_LIMIT = 63 << 20


def transform(positions):
    freq = np.arange(BLOCK)[:, None]
    angle = 2 * np.pi * ((freq * positions[None, :]) % SPAN) / SPAN
    real, imag = np.cos(angle), -np.sin(angle)
    imag[0] = np.cos(np.pi * (positions % 2))
    return np.concatenate([real, imag], axis=0)


def split(matrix):
    high = matrix.astype(np.float32).astype(BF16)
    return high, (matrix - high.astype(np.float64)).astype(np.float32).astype(BF16)


def constants():
    spread = transform(np.arange(SPAN))
    long_high, long_low = split(transform(LONG - 1 - np.arange(LONG)))
    short_table = np.zeros((SPAN, 16))
    short_table[:, :SHORT] = transform(SHORT - 1 - np.arange(SHORT))
    short_high, short_low = split(short_table)
    as_bf16 = lambda table: table.astype(np.float32).astype(BF16)
    gather_forward = as_bf16(spread[:, BLOCK:].T)
    gather_backward = as_bf16(spread[:, :BLOCK].T)
    return (
        as_bf16(spread),
        gather_forward,
        gather_backward,
        long_high,
        long_low,
        short_high,
        short_low,
    )


def layer_kernel(
    hidden,
    tokens,
    in_codes,
    in_scales,
    out_codes,
    out_scales,
    short_source,
    long_source,
    spread_source,
    gather_forward_source,
    gather_backward_source,
    long_high_source,
    long_low_source,
    short_high_source,
    short_low_source,
    gated_out,
    last_weights,
    weights,
    codes,
    last_codes,
    scales,
    last_scales,
    letters,
    token_forward,
    token_backward,
    halo_forward,
    halo_backward,
    short_filter,
    long_filter,
    spread,
    gather_forward,
    gather_backward,
    long_high,
    long_low,
    short_high,
    short_low,
    state,
    normed,
    masked_forward,
    masked_backward,
    keep,
    pure,
    cross,
    edge,
    taps,
    conv,
    load_sem,
    store_sem,
    piece_recv,
    cross_recv,
    mate_recv,
    halo_recv,
    z_send,
    y_send,
    x_send,
    mate_send,
    halo_send,
):
    dp, ctx = lax.axis_index("dp"), lax.axis_index("ctx")
    y, z_high = dp // 2, dp % 2
    z_low, x, core = ctx // 8, (ctx // 2) % 4, ctx % 2
    half = x % 2
    partner = dp + 1 - 2 * z_high
    ring = 4
    below, above, across = (y + 3) % ring, (y + 1) % ring, (y + 2) % ring
    up, down = ((dp + 2) % DP, ctx), ((dp + DP - 2) % DP, ctx)
    opposite = ((dp + 4) % DP, ctx)
    step = 1 - 2 * core

    def along_x(distance):
        return (dp, z_low * 8 + (x + ring + distance) % ring * 2 + core)

    beside = along_x(step)
    mate = (dp, ctx + step)
    after, before = (dp, (ctx + 1) % CTX), (dp, (ctx + CTX - 1) % CTX)
    border = z_low // 3 + (3 - z_low) // 3
    fetches = (core + z_high) % 2

    barrier = pltpu.get_barrier_semaphore()
    for device in (up, down, opposite, along_x(-step), mate, after, before):
        pl.semaphore_signal(barrier, inc=1, device_id=device, device_id_type=MESH)

    @pl.when(fetches == 1)
    def _():
        shift = (z_low // 2) * 24
        source = (partner, ctx + 24 - 8 * z_low - shift)
        pl.semaphore_signal(barrier, inc=1, device_id=source, device_id_type=MESH)

    loads = []

    def load(source, target):
        index = len(loads)
        copy = pltpu.make_async_copy(source, target, load_sem.at[index])
        copy.start()
        loads.append(copy)
        return copy

    code_loads = [load(in_codes, codes), load(in_scales, scales)]
    last_loads = [load(out_codes, last_codes), load(out_scales, last_scales)]
    letter_load = load(tokens, letters)
    filter_loads = [
        load(short_source, short_filter),
        load(long_source, long_filter),
        load(long_high_source, long_high),
        load(long_low_source, long_low),
        load(short_high_source, short_high),
        load(short_low_source, short_low),
    ]
    state_loads = [
        load(hidden.at[:, pl.ds(strand * WIDTH, WIDTH)], state.at[strand]) for strand in range(2)
    ]
    table_loads = [
        load(spread_source, spread),
        load(gather_forward_source, gather_forward),
        load(gather_backward_source, gather_backward),
    ]

    def base_of(row, side):
        return (2 * row + side) * SHARD

    def dequantise(part):
        for block in range(3):
            start = base_of(y, z_high) + block * 32
            rows = pl.ds(pl.multiple_of(start, 32), 32)
            for group in range(6):
                column = group * 128
                if part < 2:
                    place = part * 6 + group
                    values = codes[block, :, place * 128 : place * 128 + 128]
                    scale = scales[block : block + 1, place : place + 1]
                else:
                    values = last_codes[block, :, column : column + 128]
                    scale = last_scales[block : block + 1, group : group + 1]
                weights[part, rows, column : column + 128] = (values.astype(F32) * scale).astype(BF16)

    for copy in code_loads:
        copy.wait()
    dequantise(0)
    pl.semaphore_wait(barrier, 7 + 2 * border * (1 - fetches))

    def piece(part, row, side):
        start = base_of(row, core) + side * (SHARD // 2)
        return weights.at[part, pl.ds(pl.multiple_of(start, 16), SHARD // 2)]

    def remote(ref, device, left, received):
        return pltpu.make_async_remote_copy(
            src_ref=ref,
            dst_ref=ref,
            send_sem=left,
            recv_sem=received,
            device_id=device,
            device_id_type=MESH,
        )

    def along(part, row, device, index):
        return remote(
            piece(part, row, half), device, y_send.at[part, index], piece_recv.at[part, row]
        )

    def aside(part, row, index):
        return remote(
            piece(part, row, half),
            beside,
            x_send.at[part, index],
            cross_recv.at[part, row],
        )

    def to_mate(part, row, side, index):
        return remote(
            piece(part, row, side), mate, mate_send.at[part, index], mate_recv.at[part, row]
        )

    def z_copies(part):
        sign = 1 - 2 * (z_low // 3)
        return [
            remote(
                piece(part, y, half),
                (partner, ctx + distance * sign),
                z_send.at[part, index],
                piece_recv.at[part, y],
            )
            for index, distance in enumerate((16, 24))
        ]

    def ring_copies(part):
        return [along(part, y, up, 0), along(part, y, down, 1), along(part, y, opposite, 2)]

    def z_owner(part, action):
        @pl.when(fetches + (1 - border) == 0)
        def _():
            for copy in z_copies(part):
                action(copy)

    def ring_owner(part, action):
        @pl.when(fetches == 0)
        def _():
            for copy in ring_copies(part):
                action(copy)

    def start(copy):
        copy.start()

    def sent(copy):
        copy.wait_send()

    def relay(part):
        @pl.when(fetches == 1)
        def _():
            along(part, y, up, 0).wait_recv()
            for copy in ring_copies(part):
                copy.start()
            aside(part, y, 0).start()
            to_mate(part, y, half, 0).start()

    def collect(part):
        for index, row in enumerate((below, above, across)):
            along(part, row, up, 0).wait_recv()
            aside(part, row, index + 1).start()
            to_mate(part, row, half, 2 * index + 2).start()

    def share(part):
        def pass_on(row, index):
            remote(
                piece(part, row, 1 - half), beside, x_send.at[part, 0], cross_recv.at[part, row]
            ).wait_recv()
            to_mate(part, row, 1 - half, index).start()

        @pl.when(fetches == 1)
        def _():
            pass_on(y, 1)

        for index, row in enumerate((below, above, across)):
            pass_on(row, 2 * index + 3)

    def complete(part):
        def finish(row):
            ref = weights.at[part, pl.ds(pl.multiple_of(base_of(row, 1 - core), 32), SHARD)]
            remote(ref, mate, mate_send.at[part, 0], mate_recv.at[part, row]).wait_recv()

        @pl.when(fetches == 0)
        def _():
            finish(y)

        for row in (below, above, across):
            finish(row)

    halos = []

    def halo(source, target, device):
        index = len(halos)
        copy = pltpu.make_async_remote_copy(
            src_ref=source,
            dst_ref=target,
            send_sem=halo_send.at[index],
            recv_sem=halo_recv.at[index],
            device_id=device,
            device_id_type=MESH,
        )
        copy.start()
        halos.append(copy)

    z_owner(0, start)
    ring_owner(0, start)
    letter_load.wait()
    halo(letters.at[:, pl.ds(ROWS - 256, 256)], token_forward, after)
    halo(letters.at[:, pl.ds(0, 256)], token_backward, before)
    halo(hidden.at[pl.ds(ROWS - HALO, HALO), pl.ds(0, WIDTH)], halo_forward, after)
    halo(hidden.at[pl.ds(0, HALO), pl.ds(WIDTH, WIDTH)], halo_backward, before)
    for copy in last_loads:
        copy.wait()
    dequantise(1)
    z_owner(0, sent)
    z_owner(1, start)
    dequantise(2)

    def keep_rows(values, live):
        flags = jnp.where(values != 4, live, 0.0)
        return jnp.transpose(jnp.broadcast_to(flags, (128, 128)))

    one = jnp.float32(1.0)
    for block in range(ROWS // 128):
        keep[block * 128 + 256 : block * 128 + 384] = keep_rows(
            letters[:, block * 128 : block * 128 + 128], one
        )

    def project(values):
        wide = values.astype(F32)
        mean = jnp.mean(wide * wide, axis=-1, keepdims=True)
        return (wide * lax.rsqrt(mean + 1e-5)).astype(BF16)

    def norm_pass(tile, carry):
        rows = pl.ds(pl.multiple_of(tile * TILE, TILE), TILE)
        for strand in range(2):
            start = (2 * tile + strand) * TILE
            normed[pl.ds(pl.multiple_of(start, TILE), TILE)] = project(state[strand, rows])
        return carry

    relay(0)
    z_owner(1, sent)
    z_owner(2, start)
    for copy in state_loads:
        copy.wait()
    lax.fori_loop(0, 1, norm_pass, 0)
    relay(1)
    ring_owner(1, start)
    lax.fori_loop(1, 2, norm_pass, 0)
    relay(2)
    collect(0)
    ring_owner(2, start)
    lax.fori_loop(2, 3, norm_pass, 0)
    collect(1)
    lax.fori_loop(3, 4, norm_pass, 0)
    collect(2)
    share(0)

    for copy in filter_loads:
        copy.wait()
    short = short_filter[...].astype(F32)
    long = long_filter[...]
    padded = jnp.concatenate([short, jnp.zeros((16 - SHORT, WIDTH), F32)], axis=0).astype(BF16)
    dot = functools.partial(jnp.dot, preferred_element_type=F32)
    long_hat = dot(long_high[...], long) + dot(long_low[...], long)
    short_hat = dot(short_high[...], padded) + dot(short_low[...], padded)
    real_long, imag_long = long_hat[:BLOCK], long_hat[BLOCK:]
    real_short, imag_short = short_hat[:BLOCK], short_hat[BLOCK:]
    first = lax.broadcasted_iota(jnp.int32, (BLOCK, WIDTH), 0) == 0
    scale = jnp.where(first, 1.0 / SPAN, 2.0 / SPAN)
    reals, imags = real_short * real_long, imag_short * imag_long
    pure[...] = jnp.where(first, reals, reals - imags) * scale
    edge[...] = jnp.where(first, imags, reals - imags) * scale
    cross[...] = jnp.where(first, 0.0, real_short * imag_long + imag_short * real_long) * scale
    long_head = long[:16].astype(F32)
    taps[0:1] = short[0:1] * long_head[0:1]
    taps[1:2] = short[0:1] * long_head[1:2] + short[1:2] * long_head[0:1]

    for copy in table_loads:
        copy.wait()
    complete(0)

    def rows_in(tile):
        return pl.ds(pl.multiple_of(tile * 2 * TILE, TILE), 2 * TILE)

    def value_part(norm, flags):
        return (dot(norm, weights[0]) * jnp.tile(flags, (1, 6))).astype(BF16)

    def value_pass(tile, carry):
        start = pl.multiple_of(tile * TILE, TILE)
        rows = rows_in(tile)
        values = dot(normed[rows], weights[0])
        flags = jnp.tile(keep[pl.ds(start + 256, TILE)], (1, 6))
        masked_forward[pl.ds(pl.multiple_of(start + HALO, 16), TILE)] = (
            values[:TILE] * flags
        ).astype(BF16)
        masked_backward[pl.ds(start, TILE)] = (values[TILE:] * flags).astype(BF16)
        return carry

    lax.fori_loop(0, 2, value_pass, 0)
    share(1)
    lax.fori_loop(2, ROWS // TILE, value_pass, 0)
    share(2)

    for copy in halos:
        copy.wait_recv()
    live_before = jnp.where(ctx > 0, 1.0, 0.0)
    live_after = jnp.where(ctx < CTX - 1, 1.0, 0.0)
    for block in range(2):
        columns = slice(block * 128, block * 128 + 128)
        keep[columns] = keep_rows(token_forward[:, columns], live_before)
        keep[ROWS + 256 + block * 128 : ROWS + 384 + block * 128] = keep_rows(
            token_backward[:, columns], live_after
        )
    masked_forward[0:HALO] = value_part(project(halo_forward[...]), keep[256 - HALO : 256])
    masked_backward[ROWS : ROWS + HALO] = value_part(
        project(halo_backward[...]), keep[ROWS + 256 : ROWS + 256 + HALO]
    )
    complete(1)

    def filtered(strand, start, target):
        masked = masked_backward if strand else masked_forward
        origin = start if strand else pl.multiple_of(start + 16, 16)
        window = masked[pl.ds(origin, SPAN)]
        waves = dot(spread[...], window)
        real, imag = waves[:BLOCK], waves[BLOCK:]
        straight, turned = real * pure[...], imag * cross[...]
        upright, bent = imag * edge[...], real * cross[...]
        if strand:
            parts = [straight + turned, upright - bent]
        else:
            parts = [straight - turned, upright + bent]
        product = jnp.concatenate([part.astype(BF16) for part in parts], axis=0)
        gather = gather_backward if strand else gather_forward
        conv[target : target + BLOCK] = dot(gather[...], product)
        last, second = taps[0:1], taps[1:2]
        row = lax.broadcasted_iota(jnp.int32, (8, WIDTH), 0)
        if strand:
            wrong = masked[pl.ds(start, 16)].astype(F32)
            right = masked[pl.ds(pl.multiple_of(start + SPAN, 16), 16)].astype(F32)
            gap = right - wrong
            outer, inner = gap[0:1], gap[1:2]
            fix = jnp.where(row == 7, second * outer + last * inner, 0.0)
            fix = fix + jnp.where(row == 6, last * outer, 0.0)
            conv[target + BLOCK - 8 : target + BLOCK] += fix
        else:
            right = masked[pl.ds(start, 16)].astype(F32)
            wrong = masked[pl.ds(pl.multiple_of(start + SPAN, 16), 16)].astype(F32)
            gap = right - wrong
            outer, inner = gap[15:16], gap[14:15]
            fix = jnp.where(row == 0, second * outer + last * inner, 0.0)
            fix = fix + jnp.where(row == 1, last * outer, 0.0)
            conv[target : target + 8] += fix

    def store(tile):
        rows = rows_in(tile)
        return pltpu.make_async_copy(normed.at[rows], gated_out.at[rows], store_sem.at[tile])

    def gate_pass(tile, carry):
        start = pl.multiple_of(tile * TILE, TILE)
        rows = rows_in(tile)
        for strand in range(2):
            for block in range(TILE // BLOCK):
                offset = block * BLOCK
                filtered(strand, pl.multiple_of(start + offset, BLOCK), strand * TILE + offset)
        half_gate = 0.5 * dot(normed[rows], weights[1])
        gated = (half_gate * jnp.tanh(half_gate) + half_gate) * conv[...]
        normed[rows] = gated.astype(BF16)
        store(tile).start()
        return carry

    lax.fori_loop(0, 3, gate_pass, 0)
    complete(2)
    last_store = pltpu.make_async_copy(weights.at[2], last_weights, store_sem.at[ROWS // TILE])
    last_store.start()
    lax.fori_loop(ROWS // TILE - 1, ROWS // TILE, gate_pass, 0)

    for copy in halos:
        copy.wait_send()
    z_owner(2, sent)
    for part in range(3):
        ring_owner(part, sent)

        @pl.when(fetches == 1)
        def _(part=part):
            for copy in ring_copies(part):
                copy.wait_send()
            aside(part, y, 0).wait_send()
            for side in range(2):
                to_mate(part, y, side, side).wait_send()

        for index, row in enumerate((below, above, across)):
            aside(part, row, index + 1).wait_send()
            for side in range(2):
                to_mate(part, row, side, 2 * index + 2 + side).wait_send()
    for tile in range(ROWS // TILE):
        store(tile).wait()
    last_store.wait()


def finish_kernel(
    hidden, gated_source, weight_source, out, weight, gated, state, load_sem, ready_sem, store_sem
):
    def fetch(unit):
        rows = pl.ds(pl.multiple_of(unit * TILE, TILE), TILE)
        own = pl.ds(pl.multiple_of(unit * 2 * TILE, TILE), 2 * TILE)
        return (
            pltpu.make_async_copy(gated_source.at[own], gated.at[own], load_sem.at[unit]),
            pltpu.make_async_copy(hidden.at[rows], state.at[rows], ready_sem.at[unit]),
            pltpu.make_async_copy(state.at[rows], out.at[rows], store_sem.at[unit]),
        )

    units = ROWS // TILE
    first = pltpu.make_async_copy(weight_source, weight, load_sem.at[units])
    first.start()
    for unit in range(units):
        for copy in fetch(unit)[:2]:
            copy.start()
    first.wait()

    def out_pass(unit, carry):
        rows = pl.ds(pl.multiple_of(unit * TILE, TILE), TILE)
        own = pl.ds(pl.multiple_of(unit * 2 * TILE, TILE), 2 * TILE)
        *loads, store = fetch(unit)
        for copy in loads:
            copy.wait()
        branch = jnp.dot(gated[own], weight[...], preferred_element_type=F32)
        for strand in range(2):
            columns = slice(strand * WIDTH, strand * WIDTH + WIDTH)
            added = branch[strand * TILE : strand * TILE + TILE]
            state[rows, columns] = (state[rows, columns].astype(F32) + added).astype(BF16)
        store.start()
        return carry

    lax.fori_loop(0, units, out_pass, 0)
    for unit in range(units):
        fetch(unit)[2].wait()


def shards(
    hidden_state, tokens, in_codes, in_scales, out_codes, out_scales, short_filter, long_filter
):
    window = hidden_state[0]
    anywhere = pl.BlockSpec(memory_space=pl.ANY)
    dma = pltpu.SemaphoreType.DMA
    tables = constants()
    gated, last_weights = pl.pallas_call(
        layer_kernel,
        out_shape=(
            jax.ShapeDtypeStruct((2 * ROWS, WIDTH), BF16),
            jax.ShapeDtypeStruct((WIDTH, WIDTH), BF16),
        ),
        in_specs=[anywhere] * (8 + len(tables)),
        out_specs=(anywhere, anywhere),
        scratch_shapes=[
            pltpu.VMEM((3, WIDTH, WIDTH), BF16),
            pltpu.VMEM((3, 32, 2 * WIDTH), BF16),
            pltpu.VMEM((3, 32, WIDTH), BF16),
            pltpu.VMEM((3, 12), F32),
            pltpu.VMEM((3, 6), F32),
            pltpu.VMEM((1, ROWS), jnp.int32),
            pltpu.VMEM((1, 256), jnp.int32),
            pltpu.VMEM((1, 256), jnp.int32),
            pltpu.VMEM((HALO, WIDTH), BF16),
            pltpu.VMEM((HALO, WIDTH), BF16),
            pltpu.VMEM((SHORT, WIDTH), BF16),
            pltpu.VMEM((LONG, WIDTH), BF16),
            *(pltpu.VMEM(table.shape, BF16) for table in tables),
            pltpu.VMEM((2, ROWS, WIDTH), BF16),
            pltpu.VMEM((2 * ROWS, WIDTH), BF16),
            pltpu.VMEM((ROWS + HALO, WIDTH), BF16),
            pltpu.VMEM((ROWS + HALO, WIDTH), BF16),
            pltpu.VMEM((ROWS + 512, 128), F32),
            pltpu.VMEM((BLOCK, WIDTH), F32),
            pltpu.VMEM((BLOCK, WIDTH), F32),
            pltpu.VMEM((BLOCK, WIDTH), F32),
            pltpu.VMEM((8, WIDTH), F32),
            pltpu.VMEM((2 * TILE, WIDTH), F32),
            dma((16,)),
            dma((8,)),
            dma((3, 4)),
            dma((3, 4)),
            dma((3, 4)),
            dma((4,)),
            dma((3, 2)),
            dma((3, 3)),
            dma((3, 4)),
            dma((3, 8)),
            dma((4,)),
        ],
        compiler_params=pltpu.CompilerParams(
            collective_id=0, has_side_effects=True, vmem_limit_bytes=VMEM_LIMIT
        ),
        name="layer",
    )(
        window,
        tokens,
        in_codes,
        in_scales,
        out_codes,
        out_scales,
        short_filter,
        long_filter,
        *map(jnp.asarray, tables),
    )
    result = pl.pallas_call(
        finish_kernel,
        out_shape=jax.ShapeDtypeStruct((ROWS, 2 * WIDTH), BF16),
        in_specs=[anywhere] * 3,
        out_specs=anywhere,
        scratch_shapes=[
            pltpu.VMEM((WIDTH, WIDTH), BF16),
            pltpu.VMEM((2 * ROWS, WIDTH), BF16),
            pltpu.VMEM((ROWS, 2 * WIDTH), BF16),
            dma((8,)),
            dma((8,)),
            dma((8,)),
        ],
        compiler_params=pltpu.CompilerParams(vmem_limit_bytes=VMEM_LIMIT),
        name="finish",
    )(window, gated, last_weights)
    return result[None]


def solution(mesh):
    in_specs = (
        P("dp", "ctx", None),
        P("dp", "ctx"),
        P("dp", None, None),
        P("dp", None),
        P("dp", None, None),
        P("dp", None),
        P(),
        P(),
    )
    out_specs = P("dp", "ctx", None)
    return jax.shard_map(shards, mesh=mesh, in_specs=in_specs, out_specs=out_specs, check_vma=False)
```

```python
import functools

import jax
import jax.numpy as jnp
import numpy as np
from jax import lax
from jax.experimental import pallas as pl
from jax.experimental.pallas import tpu as pltpu
from jax.sharding import PartitionSpec as P

MESH = pl.DeviceIdType.MESH
F32, BF16 = jnp.float32, jnp.bfloat16
ROWS, HALO = 1024, 144
WIDTH, SHARD = 768, 96
BLOCK, SPAN = 128, 256
TILE, PART = 512, 256
DP, CTX = 8, 32
LONG, SHORT = 128, 4
VMEM_LIMIT = 63 << 20


def transform(positions):
    freq = np.arange(BLOCK)[:, None]
    angle = 2 * np.pi * ((freq * positions[None, :]) % SPAN) / SPAN
    real, imag = np.cos(angle), -np.sin(angle)
    imag[0] = np.cos(np.pi * (positions % 2))
    return np.concatenate([real, imag], axis=0)


def split(matrix):
    high = matrix.astype(np.float32).astype(BF16)
    return high, (matrix - high.astype(np.float64)).astype(np.float32).astype(BF16)


def constants():
    spread = transform(np.arange(SPAN))
    long_high, long_low = split(transform(LONG - 1 - np.arange(LONG)))
    short_table = np.zeros((SPAN, 16))
    short_table[:, :SHORT] = transform(SHORT - 1 - np.arange(SHORT))
    short_high, short_low = split(short_table)
    as_bf16 = lambda table: table.astype(np.float32).astype(BF16)
    gather_forward = as_bf16(spread[:, BLOCK:].T)
    gather_backward = as_bf16(spread[:, :BLOCK].T)
    return (
        as_bf16(spread),
        gather_forward,
        gather_backward,
        long_high,
        long_low,
        short_high,
        short_low,
    )


def layer_kernel(
    hidden,
    tokens,
    in_codes,
    in_scales,
    out_codes,
    out_scales,
    short_source,
    long_source,
    spread_source,
    gather_forward_source,
    gather_backward_source,
    long_high_source,
    long_low_source,
    short_high_source,
    short_low_source,
    gated_out,
    last_weights,
    weights,
    codes,
    last_codes,
    scales,
    last_scales,
    letters,
    token_forward,
    token_backward,
    halo_forward,
    halo_backward,
    short_filter,
    long_filter,
    spread,
    gather_forward,
    gather_backward,
    long_high,
    long_low,
    short_high,
    short_low,
    state,
    normed,
    masked_forward,
    masked_backward,
    keep,
    pure,
    cross,
    edge,
    taps,
    conv,
    load_sem,
    store_sem,
    piece_recv,
    cross_recv,
    mate_recv,
    halo_recv,
    z_send,
    y_send,
    x_send,
    mate_send,
    halo_send,
):
    dp, ctx = lax.axis_index("dp"), lax.axis_index("ctx")
    y, z_high = dp // 2, dp % 2
    z_low, x, core = ctx // 8, (ctx // 2) % 4, ctx % 2
    half = x % 2
    partner = dp + 1 - 2 * z_high
    ring = 4
    below, above, across = (y + 3) % ring, (y + 1) % ring, (y + 2) % ring
    up, down = ((dp + 2) % DP, ctx), ((dp + DP - 2) % DP, ctx)
    opposite = ((dp + 4) % DP, ctx)
    step = 1 - 2 * core

    def along_x(distance):
        return (dp, z_low * 8 + (x + ring + distance) % ring * 2 + core)

    beside = along_x(step)
    mate = (dp, ctx + step)
    after, before = (dp, (ctx + 1) % CTX), (dp, (ctx + CTX - 1) % CTX)
    border = z_low // 3 + (3 - z_low) // 3
    fetches = (core + z_high) % 2

    barrier = pltpu.get_barrier_semaphore()
    for device in (up, down, opposite, along_x(-step), mate, after, before):
        pl.semaphore_signal(barrier, inc=1, device_id=device, device_id_type=MESH)

    @pl.when(fetches == 1)
    def _():
        shift = (z_low // 2) * 24
        source = (partner, ctx + 24 - 8 * z_low - shift)
        pl.semaphore_signal(barrier, inc=1, device_id=source, device_id_type=MESH)

    loads = []

    def load(source, target):
        index = len(loads)
        copy = pltpu.make_async_copy(source, target, load_sem.at[index])
        copy.start()
        loads.append(copy)
        return copy

    code_loads = [load(in_codes, codes), load(in_scales, scales)]
    last_loads = [load(out_codes, last_codes), load(out_scales, last_scales)]
    letter_load = load(tokens, letters)
    filter_loads = [
        load(short_source, short_filter),
        load(long_source, long_filter),
        load(long_high_source, long_high),
        load(long_low_source, long_low),
        load(short_high_source, short_high),
        load(short_low_source, short_low),
    ]
    state_loads = [
        load(hidden.at[:, pl.ds(strand * WIDTH, WIDTH)], state.at[strand]) for strand in range(2)
    ]
    table_loads = [
        load(spread_source, spread),
        load(gather_forward_source, gather_forward),
        load(gather_backward_source, gather_backward),
    ]

    def base_of(row, side):
        return (2 * row + side) * SHARD

    def dequantise(part):
        for block in range(3):
            start = base_of(y, z_high) + block * 32
            rows = pl.ds(pl.multiple_of(start, 32), 32)
            for group in range(6):
                column = group * 128
                if part < 2:
                    place = part * 6 + group
                    values = codes[block, :, place * 128 : place * 128 + 128]
                    scale = scales[block : block + 1, place : place + 1]
                else:
                    values = last_codes[block, :, column : column + 128]
                    scale = last_scales[block : block + 1, group : group + 1]
                weights[part, rows, column : column + 128] = (values.astype(F32) * scale).astype(BF16)

    for copy in code_loads:
        copy.wait()
    dequantise(0)
    pl.semaphore_wait(barrier, 7 + 2 * border * (1 - fetches))

    def piece(part, row, side):
        start = base_of(row, core) + side * (SHARD // 2)
        return weights.at[part, pl.ds(pl.multiple_of(start, 16), SHARD // 2)]

    def remote(ref, device, left, received):
        return pltpu.make_async_remote_copy(
            src_ref=ref,
            dst_ref=ref,
            send_sem=left,
            recv_sem=received,
            device_id=device,
            device_id_type=MESH,
        )

    def along(part, row, device, index):
        return remote(
            piece(part, row, half), device, y_send.at[part, index], piece_recv.at[part, row]
        )

    def aside(part, row, index):
        return remote(
            piece(part, row, half),
            beside,
            x_send.at[part, index],
            cross_recv.at[part, row],
        )

    def to_mate(part, row, side, index):
        return remote(
            piece(part, row, side), mate, mate_send.at[part, index], mate_recv.at[part, row]
        )

    def z_copies(part):
        sign = 1 - 2 * (z_low // 3)
        return [
            remote(
                piece(part, y, half),
                (partner, ctx + distance * sign),
                z_send.at[part, index],
                piece_recv.at[part, y],
            )
            for index, distance in enumerate((16, 24))
        ]

    def ring_copies(part):
        return [along(part, y, up, 0), along(part, y, down, 1), along(part, y, opposite, 2)]

    def z_owner(part, action):
        @pl.when(fetches + (1 - border) == 0)
        def _():
            for copy in z_copies(part):
                action(copy)

    def ring_owner(part, action):
        @pl.when(fetches == 0)
        def _():
            for copy in ring_copies(part):
                action(copy)

    def start(copy):
        copy.start()

    def sent(copy):
        copy.wait_send()

    def relay(part):
        @pl.when(fetches == 1)
        def _():
            along(part, y, up, 0).wait_recv()
            for copy in ring_copies(part):
                copy.start()
            aside(part, y, 0).start()
            to_mate(part, y, half, 0).start()

    def collect(part):
        for index, row in enumerate((below, above, across)):
            along(part, row, up, 0).wait_recv()
            aside(part, row, index + 1).start()
            to_mate(part, row, half, 2 * index + 2).start()

    def share(part):
        def pass_on(row, index):
            remote(
                piece(part, row, 1 - half), beside, x_send.at[part, 0], cross_recv.at[part, row]
            ).wait_recv()
            to_mate(part, row, 1 - half, index).start()

        @pl.when(fetches == 1)
        def _():
            pass_on(y, 1)

        for index, row in enumerate((below, above, across)):
            pass_on(row, 2 * index + 3)

    def complete(part):
        def finish(row):
            ref = weights.at[part, pl.ds(pl.multiple_of(base_of(row, 1 - core), 32), SHARD)]
            remote(ref, mate, mate_send.at[part, 0], mate_recv.at[part, row]).wait_recv()

        @pl.when(fetches == 0)
        def _():
            finish(y)

        for row in (below, above, across):
            finish(row)

    halos = []

    def halo(source, target, device):
        index = len(halos)
        copy = pltpu.make_async_remote_copy(
            src_ref=source,
            dst_ref=target,
            send_sem=halo_send.at[index],
            recv_sem=halo_recv.at[index],
            device_id=device,
            device_id_type=MESH,
        )
        copy.start()
        halos.append(copy)

    z_owner(0, start)
    ring_owner(0, start)
    letter_load.wait()
    halo(letters.at[:, pl.ds(ROWS - 256, 256)], token_forward, after)
    halo(letters.at[:, pl.ds(0, 256)], token_backward, before)
    halo(hidden.at[pl.ds(ROWS - HALO, HALO), pl.ds(0, WIDTH)], halo_forward, after)
    halo(hidden.at[pl.ds(0, HALO), pl.ds(WIDTH, WIDTH)], halo_backward, before)
    for copy in last_loads:
        copy.wait()
    dequantise(1)
    z_owner(0, sent)
    z_owner(1, start)
    dequantise(2)

    def keep_rows(values, live):
        flags = jnp.where(values != 4, live, 0.0)
        return jnp.transpose(jnp.broadcast_to(flags, (128, 128)))

    one = jnp.float32(1.0)
    for block in range(ROWS // 128):
        keep[block * 128 + 256 : block * 128 + 384] = keep_rows(
            letters[:, block * 128 : block * 128 + 128], one
        )

    def project(values):
        wide = values.astype(F32)
        mean = jnp.mean(wide * wide, axis=-1, keepdims=True)
        return (wide * lax.rsqrt(mean + 1e-5)).astype(BF16)

    def norm_pass(part, carry):
        rows = pl.ds(pl.multiple_of(part * PART, PART), PART)
        for strand in range(2):
            start = part // 2 * (2 * TILE) + strand * TILE + part % 2 * PART
            normed[pl.ds(pl.multiple_of(start, PART), PART)] = project(state[strand, rows])
        return carry

    relay(0)
    z_owner(1, sent)
    z_owner(2, start)
    for copy in state_loads:
        copy.wait()
    lax.fori_loop(0, 1, norm_pass, 0)
    relay(1)
    ring_owner(1, start)
    lax.fori_loop(1, 2, norm_pass, 0)
    relay(2)
    collect(0)
    ring_owner(2, start)
    lax.fori_loop(2, 3, norm_pass, 0)
    collect(1)
    lax.fori_loop(3, 4, norm_pass, 0)
    collect(2)
    share(0)

    for copy in filter_loads:
        copy.wait()
    short = short_filter[...].astype(F32)
    long = long_filter[...]
    padded = jnp.concatenate([short, jnp.zeros((16 - SHORT, WIDTH), F32)], axis=0).astype(BF16)
    dot = functools.partial(jnp.dot, preferred_element_type=F32)
    long_hat = dot(long_high[...], long) + dot(long_low[...], long)
    short_hat = dot(short_high[...], padded) + dot(short_low[...], padded)
    real_long, imag_long = long_hat[:BLOCK], long_hat[BLOCK:]
    real_short, imag_short = short_hat[:BLOCK], short_hat[BLOCK:]
    first = lax.broadcasted_iota(jnp.int32, (BLOCK, WIDTH), 0) == 0
    scale = jnp.where(first, 1.0 / SPAN, 2.0 / SPAN)
    reals, imags = real_short * real_long, imag_short * imag_long
    pure[...] = jnp.where(first, reals, reals - imags) * scale
    edge[...] = jnp.where(first, imags, reals - imags) * scale
    cross[...] = jnp.where(first, 0.0, real_short * imag_long + imag_short * real_long) * scale
    long_head = long[:16].astype(F32)
    taps[0:1] = short[0:1] * long_head[0:1]
    taps[1:2] = short[0:1] * long_head[1:2] + short[1:2] * long_head[0:1]

    for copy in table_loads:
        copy.wait()
    complete(0)

    def value_tile(tile, count):
        start = tile * TILE
        values = dot(normed[2 * start : 2 * start + count], weights[0])
        flags = jnp.tile(keep[start + 256 : start + 256 + TILE], (1, 6))
        masked_forward[start + HALO : start + HALO + TILE] = (values[:TILE] * flags).astype(BF16)
        masked_backward[start : start + TILE] = (values[TILE : 2 * TILE] * flags).astype(BF16)
        return values[2 * TILE :]

    value_tile(0, 2 * TILE)
    share(1)
    for copy in halos:
        copy.wait_recv()
    live_before = jnp.where(ctx > 0, 1.0, 0.0)
    live_after = jnp.where(ctx < CTX - 1, 1.0, 0.0)
    for block in range(2):
        columns = slice(block * 128, block * 128 + 128)
        keep[columns] = keep_rows(token_forward[:, columns], live_before)
        keep[ROWS + 256 + block * 128 : ROWS + 384 + block * 128] = keep_rows(
            token_backward[:, columns], live_after
        )
    normed[2 * ROWS : 2 * ROWS + HALO] = project(halo_forward[...])
    normed[2 * ROWS + HALO :] = project(halo_backward[...])
    rims = value_tile(1, 2 * TILE + 2 * HALO)
    masked_forward[:HALO] = (rims[:HALO] * jnp.tile(keep[256 - HALO : 256], (1, 6))).astype(BF16)
    masked_backward[ROWS:] = (
        rims[HALO:] * jnp.tile(keep[ROWS + 256 : ROWS + 256 + HALO], (1, 6))
    ).astype(BF16)

    def filtered(strand, start, target):
        masked = masked_backward if strand else masked_forward
        origin = start if strand else start + 16
        window = masked[pl.ds(origin, SPAN)]
        waves = dot(spread[...], window)
        real, imag = waves[:BLOCK], waves[BLOCK:]
        straight, turned = real * pure[...], imag * cross[...]
        upright, bent = imag * edge[...], real * cross[...]
        if strand:
            parts = [straight + turned, upright - bent]
        else:
            parts = [straight - turned, upright + bent]
        product = jnp.concatenate([part.astype(BF16) for part in parts], axis=0)
        gather = gather_backward if strand else gather_forward
        conv[target : target + BLOCK] = dot(gather[...], product)
        last, second = taps[0:1], taps[1:2]
        row = lax.broadcasted_iota(jnp.int32, (8, WIDTH), 0)
        if strand:
            wrong = masked[pl.ds(start, 16)].astype(F32)
            right = masked[pl.ds(start + SPAN, 16)].astype(F32)
            gap = right - wrong
            outer, inner = gap[0:1], gap[1:2]
            fix = jnp.where(row == 7, second * outer + last * inner, 0.0)
            fix = fix + jnp.where(row == 6, last * outer, 0.0)
            conv[target + BLOCK - 8 : target + BLOCK] += fix
        else:
            right = masked[pl.ds(start, 16)].astype(F32)
            wrong = masked[pl.ds(start + SPAN, 16)].astype(F32)
            gap = right - wrong
            outer, inner = gap[15:16], gap[14:15]
            fix = jnp.where(row == 0, second * outer + last * inner, 0.0)
            fix = fix + jnp.where(row == 1, last * outer, 0.0)
            conv[target : target + 8] += fix

    def store(tile):
        rows = pl.ds(tile * 2 * TILE, 2 * TILE)
        return pltpu.make_async_copy(normed.at[rows], gated_out.at[rows], store_sem.at[tile])

    def conv_tile(tile):
        for strand in range(2):
            for offset in range(0, TILE, BLOCK):
                filtered(strand, tile * TILE + offset, strand * TILE + offset)

    def gate_tile(tile):
        rows = slice(tile * 2 * TILE, (tile + 1) * 2 * TILE)
        half_gate = 0.5 * dot(normed[rows], weights[1])
        gated = (half_gate * jnp.tanh(half_gate) + half_gate) * conv[...]
        normed[rows] = gated.astype(BF16)
        store(tile).start()

    conv_tile(0)
    share(2)
    complete(1)
    gate_tile(0)
    conv_tile(1)
    complete(2)
    last_store = pltpu.make_async_copy(weights.at[2], last_weights, store_sem.at[ROWS // TILE])
    last_store.start()
    gate_tile(1)

    for copy in halos:
        copy.wait_send()
    z_owner(2, sent)
    for part in range(3):
        ring_owner(part, sent)

        @pl.when(fetches == 1)
        def _(part=part):
            for copy in ring_copies(part):
                copy.wait_send()
            aside(part, y, 0).wait_send()
            for side in range(2):
                to_mate(part, y, side, side).wait_send()

        for index, row in enumerate((below, above, across)):
            aside(part, row, index + 1).wait_send()
            for side in range(2):
                to_mate(part, row, side, 2 * index + 2 + side).wait_send()
    for tile in range(ROWS // TILE):
        store(tile).wait()
    last_store.wait()


def finish_kernel(
    hidden, gated_source, weight_source, out, weight, gated, state, load_sem, ready_sem, store_sem
):
    def fetch(unit):
        rows = pl.ds(pl.multiple_of(unit * PART, PART), PART)
        own = pl.multiple_of(unit * 2 * PART, PART)
        loads = [pltpu.make_async_copy(hidden.at[rows], state.at[rows], ready_sem.at[unit])]
        for strand in range(2):
            start = unit // 2 * (2 * TILE) + strand * TILE + unit % 2 * PART
            loads.append(
                pltpu.make_async_copy(
                    gated_source.at[pl.ds(pl.multiple_of(start, PART), PART)],
                    gated.at[pl.ds(own + strand * PART, PART)],
                    load_sem.at[unit, strand],
                )
            )
        return *loads, pltpu.make_async_copy(state.at[rows], out.at[rows], store_sem.at[unit])

    units = ROWS // PART
    first = pltpu.make_async_copy(weight_source, weight, load_sem.at[units, 0])
    first.start()
    for unit in range(units):
        for copy in fetch(unit)[:-1]:
            copy.start()
    first.wait()

    def out_pass(unit, carry):
        rows = pl.ds(pl.multiple_of(unit * PART, PART), PART)
        own = pl.ds(pl.multiple_of(unit * 2 * PART, PART), 2 * PART)
        *loads, store = fetch(unit)
        for copy in loads:
            copy.wait()
        branch = jnp.dot(gated[own], weight[...], preferred_element_type=F32)
        for strand in range(2):
            columns = slice(strand * WIDTH, strand * WIDTH + WIDTH)
            added = branch[strand * PART : strand * PART + PART]
            state[rows, columns] = (state[rows, columns].astype(F32) + added).astype(BF16)
        store.start()
        return carry

    lax.fori_loop(0, units, out_pass, 0)
    for unit in range(units):
        fetch(unit)[-1].wait()


def shards(
    hidden_state, tokens, in_codes, in_scales, out_codes, out_scales, short_filter, long_filter
):
    window = hidden_state[0]
    anywhere = pl.BlockSpec(memory_space=pl.ANY)
    dma = pltpu.SemaphoreType.DMA
    tables = constants()
    gated, last_weights = pl.pallas_call(
        layer_kernel,
        out_shape=(
            jax.ShapeDtypeStruct((2 * ROWS, WIDTH), BF16),
            jax.ShapeDtypeStruct((WIDTH, WIDTH), BF16),
        ),
        in_specs=[anywhere] * (8 + len(tables)),
        out_specs=(anywhere, anywhere),
        scratch_shapes=[
            pltpu.VMEM((3, WIDTH, WIDTH), BF16),
            pltpu.VMEM((3, 32, 2 * WIDTH), BF16),
            pltpu.VMEM((3, 32, WIDTH), BF16),
            pltpu.VMEM((3, 12), F32),
            pltpu.VMEM((3, 6), F32),
            pltpu.VMEM((1, ROWS), jnp.int32),
            pltpu.VMEM((1, 256), jnp.int32),
            pltpu.VMEM((1, 256), jnp.int32),
            pltpu.VMEM((HALO, WIDTH), BF16),
            pltpu.VMEM((HALO, WIDTH), BF16),
            pltpu.VMEM((SHORT, WIDTH), BF16),
            pltpu.VMEM((LONG, WIDTH), BF16),
            *(pltpu.VMEM(table.shape, BF16) for table in tables),
            pltpu.VMEM((2, ROWS, WIDTH), BF16),
            pltpu.VMEM((2 * ROWS + 2 * HALO, WIDTH), BF16),
            pltpu.VMEM((ROWS + HALO, WIDTH), BF16),
            pltpu.VMEM((ROWS + HALO, WIDTH), BF16),
            pltpu.VMEM((ROWS + 512, 128), F32),
            pltpu.VMEM((BLOCK, WIDTH), F32),
            pltpu.VMEM((BLOCK, WIDTH), F32),
            pltpu.VMEM((BLOCK, WIDTH), F32),
            pltpu.VMEM((8, WIDTH), F32),
            pltpu.VMEM((2 * TILE, WIDTH), F32),
            dma((16,)),
            dma((8,)),
            dma((3, 4)),
            dma((3, 4)),
            dma((3, 4)),
            dma((4,)),
            dma((3, 2)),
            dma((3, 3)),
            dma((3, 4)),
            dma((3, 8)),
            dma((4,)),
        ],
        compiler_params=pltpu.CompilerParams(
            collective_id=0, has_side_effects=True, vmem_limit_bytes=VMEM_LIMIT
        ),
        name="layer",
    )(
        window,
        tokens,
        in_codes,
        in_scales,
        out_codes,
        out_scales,
        short_filter,
        long_filter,
        *map(jnp.asarray, tables),
    )
    result = pl.pallas_call(
        finish_kernel,
        out_shape=jax.ShapeDtypeStruct((ROWS, 2 * WIDTH), BF16),
        in_specs=[anywhere] * 3,
        out_specs=anywhere,
        scratch_shapes=[
            pltpu.VMEM((WIDTH, WIDTH), BF16),
            pltpu.VMEM((2 * ROWS, WIDTH), BF16),
            pltpu.VMEM((ROWS, 2 * WIDTH), BF16),
            dma((ROWS // PART + 1, 2)),
            dma((8,)),
            dma((8,)),
        ],
        compiler_params=pltpu.CompilerParams(vmem_limit_bytes=VMEM_LIMIT),
        name="finish",
    )(window, gated, last_weights)
    return result[None]


def solution(mesh):
    in_specs = (
        P("dp", "ctx", None),
        P("dp", "ctx"),
        P("dp", None, None),
        P("dp", None),
        P("dp", None, None),
        P("dp", None),
        P(),
        P(),
    )
    out_specs = P("dp", "ctx", None)
    return jax.shard_map(shards, mesh=mesh, in_specs=in_specs, out_specs=out_specs, check_vma=False)
```

```python
import functools

import jax
import jax.numpy as jnp
import numpy as np
from jax import lax
from jax.experimental import pallas as pl
from jax.experimental.pallas import tpu as pltpu
from jax.sharding import PartitionSpec as P

MESH = pl.DeviceIdType.MESH
F32, BF16 = jnp.float32, jnp.bfloat16
ROWS, HALO = 1024, 144
WIDTH, SHARD = 768, 96
BLOCK, SPAN = 128, 256
TILE, PART = 512, 256
DP, CTX = 8, 32
LONG, SHORT = 128, 4
VMEM_LIMIT = 63 << 20


def transform(positions):
    freq = np.arange(BLOCK)[:, None]
    angle = 2 * np.pi * ((freq * positions[None, :]) % SPAN) / SPAN
    real, imag = np.cos(angle), -np.sin(angle)
    imag[0] = np.cos(np.pi * (positions % 2))
    return np.concatenate([real, imag], axis=0)


def split(matrix):
    high = matrix.astype(np.float32).astype(BF16)
    return high, (matrix - high.astype(np.float64)).astype(np.float32).astype(BF16)


def constants():
    spread = transform(np.arange(SPAN))
    long_high, long_low = split(transform(LONG - 1 - np.arange(LONG)))
    short_table = np.zeros((SPAN, 16))
    short_table[:, :SHORT] = transform(SHORT - 1 - np.arange(SHORT))
    short_high, short_low = split(short_table)
    as_bf16 = lambda table: table.astype(np.float32).astype(BF16)
    gather_forward = as_bf16(spread[:, BLOCK:].T)
    gather_backward = as_bf16(spread[:, :BLOCK].T)
    return (
        as_bf16(spread),
        gather_forward,
        gather_backward,
        long_high,
        long_low,
        short_high,
        short_low,
    )


def layer_kernel(
    hidden,
    tokens,
    in_codes,
    in_scales,
    out_codes,
    out_scales,
    short_source,
    long_source,
    spread_source,
    gather_forward_source,
    gather_backward_source,
    long_high_source,
    long_low_source,
    short_high_source,
    short_low_source,
    gated_out,
    last_weights,
    weights,
    codes,
    last_codes,
    scales,
    last_scales,
    letters,
    token_forward,
    token_backward,
    halo_forward,
    halo_backward,
    short_filter,
    long_filter,
    spread,
    gather_forward,
    gather_backward,
    long_high,
    long_low,
    short_high,
    short_low,
    state,
    normed,
    masked_forward,
    masked_backward,
    keep,
    pure,
    cross,
    edge,
    taps,
    conv,
    load_sem,
    store_sem,
    piece_recv,
    cross_recv,
    mate_recv,
    halo_recv,
    z_send,
    y_send,
    x_send,
    mate_send,
    halo_send,
):
    dp, ctx = lax.axis_index("dp"), lax.axis_index("ctx")
    y, z_high = dp // 2, dp % 2
    z_low, x, core = ctx // 8, (ctx // 2) % 4, ctx % 2
    half = x % 2
    partner = dp + 1 - 2 * z_high
    ring = 4
    below, above, across = (y + 3) % ring, (y + 1) % ring, (y + 2) % ring
    up, down = ((dp + 2) % DP, ctx), ((dp + DP - 2) % DP, ctx)
    opposite = ((dp + 4) % DP, ctx)
    step = 1 - 2 * core

    def along_x(distance):
        return (dp, z_low * 8 + (x + ring + distance) % ring * 2 + core)

    beside = along_x(step)
    mate = (dp, ctx + step)
    after, before = (dp, (ctx + 1) % CTX), (dp, (ctx + CTX - 1) % CTX)
    border = z_low // 3 + (3 - z_low) // 3
    fetches = (core + z_high) % 2

    barrier = pltpu.get_barrier_semaphore()
    for device in (up, down, opposite, along_x(-step), mate, after, before):
        pl.semaphore_signal(barrier, inc=1, device_id=device, device_id_type=MESH)

    @pl.when(fetches == 1)
    def _():
        shift = (z_low // 2) * 24
        source = (partner, ctx + 24 - 8 * z_low - shift)
        pl.semaphore_signal(barrier, inc=1, device_id=source, device_id_type=MESH)

    loads = []

    def load(source, target):
        index = len(loads)
        copy = pltpu.make_async_copy(source, target, load_sem.at[index])
        copy.start()
        loads.append(copy)
        return copy

    code_loads = [load(in_codes, codes), load(in_scales, scales)]
    last_loads = [load(out_codes, last_codes), load(out_scales, last_scales)]
    letter_load = load(tokens, letters)
    filter_loads = [
        load(short_source, short_filter),
        load(long_source, long_filter),
        load(long_high_source, long_high),
        load(long_low_source, long_low),
        load(short_high_source, short_high),
        load(short_low_source, short_low),
    ]
    state_loads = [
        load(hidden.at[:, pl.ds(strand * WIDTH, WIDTH)], state.at[strand]) for strand in range(2)
    ]
    table_loads = [
        load(spread_source, spread),
        load(gather_forward_source, gather_forward),
        load(gather_backward_source, gather_backward),
    ]

    def base_of(row, side):
        return (2 * row + side) * SHARD

    def dequantise(part):
        for block in range(3):
            start = base_of(y, z_high) + block * 32
            rows = pl.ds(pl.multiple_of(start, 32), 32)
            for group in range(6):
                column = group * 128
                if part < 2:
                    place = part * 6 + group
                    values = codes[block, :, place * 128 : place * 128 + 128]
                    scale = scales[block : block + 1, place : place + 1]
                else:
                    values = last_codes[block, :, column : column + 128]
                    scale = last_scales[block : block + 1, group : group + 1]
                weights[part, rows, column : column + 128] = (values.astype(F32) * scale).astype(BF16)

    for copy in code_loads:
        copy.wait()
    dequantise(0)
    pl.semaphore_wait(barrier, 7 + 2 * border * (1 - fetches))

    def piece(part, row, side):
        start = base_of(row, core) + side * (SHARD // 2)
        return weights.at[part, pl.ds(pl.multiple_of(start, 16), SHARD // 2)]

    def remote(ref, device, left, received):
        return pltpu.make_async_remote_copy(
            src_ref=ref,
            dst_ref=ref,
            send_sem=left,
            recv_sem=received,
            device_id=device,
            device_id_type=MESH,
        )

    def along(part, row, device, index):
        return remote(
            piece(part, row, half), device, y_send.at[part, index], piece_recv.at[part, row]
        )

    def aside(part, row, index):
        return remote(
            piece(part, row, half),
            beside,
            x_send.at[part, index],
            cross_recv.at[part, row],
        )

    def to_mate(part, row, index):
        ref = weights.at[part, pl.ds(pl.multiple_of(base_of(row, core), 32), SHARD)]
        return remote(ref, mate, mate_send.at[part, index], mate_recv.at[part, row])

    def z_copies(part):
        sign = 1 - 2 * (z_low // 3)
        return [
            remote(
                piece(part, y, half),
                (partner, ctx + distance * sign),
                z_send.at[part, index],
                piece_recv.at[part, y],
            )
            for index, distance in enumerate((16, 24))
        ]

    def ring_copies(part):
        return [along(part, y, up, 0), along(part, y, down, 1), along(part, y, opposite, 2)]

    def z_owner(part, action):
        @pl.when(fetches + (1 - border) == 0)
        def _():
            for copy in z_copies(part):
                action(copy)

    def ring_owner(part, action):
        @pl.when(fetches == 0)
        def _():
            for copy in ring_copies(part):
                action(copy)

    def start(copy):
        copy.start()

    def sent(copy):
        copy.wait_send()

    def relay(part):
        @pl.when(fetches == 1)
        def _():
            along(part, y, up, 0).wait_recv()
            for copy in ring_copies(part):
                copy.start()
            aside(part, y, 0).start()

    def collect(part):
        for index, row in enumerate((below, above, across)):
            along(part, row, up, 0).wait_recv()
            aside(part, row, index + 1).start()

    def share(part):
        def pass_on(row, index):
            remote(
                piece(part, row, 1 - half), beside, x_send.at[part, 0], cross_recv.at[part, row]
            ).wait_recv()
            to_mate(part, row, index).start()

        @pl.when(fetches == 1)
        def _():
            pass_on(y, 0)

        for index, row in enumerate((below, above, across)):
            pass_on(row, index + 1)

    def complete(part):
        def finish(row):
            ref = weights.at[part, pl.ds(pl.multiple_of(base_of(row, 1 - core), 32), SHARD)]
            remote(ref, mate, mate_send.at[part, 0], mate_recv.at[part, row]).wait_recv()

        @pl.when(fetches == 0)
        def _():
            finish(y)

        for row in (below, above, across):
            finish(row)

    halos = []

    def halo(source, target, device):
        index = len(halos)
        copy = pltpu.make_async_remote_copy(
            src_ref=source,
            dst_ref=target,
            send_sem=halo_send.at[index],
            recv_sem=halo_recv.at[index],
            device_id=device,
            device_id_type=MESH,
        )
        copy.start()
        halos.append(copy)

    def open_part(part):
        z_owner(part, start)
        ring_owner(part, start)

    open_part(0)
    for copy in last_loads:
        copy.wait()
    dequantise(1)
    open_part(1)
    dequantise(2)
    open_part(2)
    letter_load.wait()
    halo(letters.at[:, pl.ds(ROWS - 256, 256)], token_forward, after)
    halo(letters.at[:, pl.ds(0, 256)], token_backward, before)
    halo(hidden.at[pl.ds(ROWS - HALO, HALO), pl.ds(0, WIDTH)], halo_forward, after)
    halo(hidden.at[pl.ds(0, HALO), pl.ds(WIDTH, WIDTH)], halo_backward, before)

    def keep_rows(values, live):
        flags = jnp.where(values != 4, live, 0.0)
        return jnp.transpose(jnp.broadcast_to(flags, (128, 128)))

    one = jnp.float32(1.0)
    for block in range(ROWS // 128):
        keep[block * 128 + 256 : block * 128 + 384] = keep_rows(
            letters[:, block * 128 : block * 128 + 128], one
        )

    def project(values):
        wide = values.astype(F32)
        mean = jnp.mean(wide * wide, axis=-1, keepdims=True)
        return (wide * lax.rsqrt(mean + 1e-5)).astype(BF16)

    def norm_pass(part, carry):
        rows = pl.ds(pl.multiple_of(part * PART, PART), PART)
        for strand in range(2):
            start = part // 2 * (2 * TILE) + strand * TILE + part % 2 * PART
            normed[pl.ds(pl.multiple_of(start, PART), PART)] = project(state[strand, rows])
        return carry

    for copy in state_loads:
        copy.wait()
    lax.fori_loop(0, 1, norm_pass, 0)
    relay(0)
    lax.fori_loop(1, 3, norm_pass, 0)
    relay(1)
    lax.fori_loop(3, 4, norm_pass, 0)
    relay(2)
    collect(0)
    collect(1)

    for copy in filter_loads:
        copy.wait()
    short = short_filter[...].astype(F32)
    long = long_filter[...]
    padded = jnp.concatenate([short, jnp.zeros((16 - SHORT, WIDTH), F32)], axis=0).astype(BF16)
    dot = functools.partial(jnp.dot, preferred_element_type=F32)
    long_hat = dot(long_high[...], long) + dot(long_low[...], long)
    short_hat = dot(short_high[...], padded) + dot(short_low[...], padded)
    real_long, imag_long = long_hat[:BLOCK], long_hat[BLOCK:]
    real_short, imag_short = short_hat[:BLOCK], short_hat[BLOCK:]
    first = lax.broadcasted_iota(jnp.int32, (BLOCK, WIDTH), 0) == 0
    scale = jnp.where(first, 1.0 / SPAN, 2.0 / SPAN)
    reals, imags = real_short * real_long, imag_short * imag_long
    pure[...] = jnp.where(first, reals, reals - imags) * scale
    edge[...] = jnp.where(first, imags, reals - imags) * scale
    cross[...] = jnp.where(first, 0.0, real_short * imag_long + imag_short * real_long) * scale
    long_head = long[:16].astype(F32)
    taps[0:1] = short[0:1] * long_head[0:1]
    taps[1:2] = short[0:1] * long_head[1:2] + short[1:2] * long_head[0:1]

    for copy in table_loads:
        copy.wait()
    share(0)
    collect(2)
    complete(0)

    def value_tile(tile, count):
        start = tile * TILE
        values = dot(normed[2 * start : 2 * start + count], weights[0])
        flags = jnp.tile(keep[start + 256 : start + 256 + TILE], (1, 6))
        masked_forward[start + HALO : start + HALO + TILE] = (values[:TILE] * flags).astype(BF16)
        masked_backward[start : start + TILE] = (values[TILE : 2 * TILE] * flags).astype(BF16)
        return values[2 * TILE :]

    value_tile(0, 2 * TILE)
    share(1)
    share(2)
    for copy in halos:
        copy.wait_recv()
    live_before = jnp.where(ctx > 0, 1.0, 0.0)
    live_after = jnp.where(ctx < CTX - 1, 1.0, 0.0)
    for block in range(2):
        columns = slice(block * 128, block * 128 + 128)
        keep[columns] = keep_rows(token_forward[:, columns], live_before)
        keep[ROWS + 256 + block * 128 : ROWS + 384 + block * 128] = keep_rows(
            token_backward[:, columns], live_after
        )
    normed[2 * ROWS : 2 * ROWS + HALO] = project(halo_forward[...])
    normed[2 * ROWS + HALO :] = project(halo_backward[...])
    rims = value_tile(1, 2 * TILE + 2 * HALO)
    masked_forward[:HALO] = (rims[:HALO] * jnp.tile(keep[256 - HALO : 256], (1, 6))).astype(BF16)
    masked_backward[ROWS:] = (
        rims[HALO:] * jnp.tile(keep[ROWS + 256 : ROWS + 256 + HALO], (1, 6))
    ).astype(BF16)

    def filtered(strand, start, target):
        masked = masked_backward if strand else masked_forward
        origin = start if strand else pl.multiple_of(start + 16, 16)
        window = masked[pl.ds(origin, SPAN)]
        waves = dot(spread[...], window)
        real, imag = waves[:BLOCK], waves[BLOCK:]
        straight, turned = real * pure[...], imag * cross[...]
        upright, bent = imag * edge[...], real * cross[...]
        if strand:
            parts = [straight + turned, upright - bent]
        else:
            parts = [straight - turned, upright + bent]
        product = jnp.concatenate([part.astype(BF16) for part in parts], axis=0)
        gather = gather_backward if strand else gather_forward
        conv[target : target + BLOCK] = dot(gather[...], product)
        last, second = taps[0:1], taps[1:2]
        row = lax.broadcasted_iota(jnp.int32, (8, WIDTH), 0)
        if strand:
            wrong = masked[pl.ds(start, 16)].astype(F32)
            right = masked[pl.ds(pl.multiple_of(start + SPAN, 16), 16)].astype(F32)
            gap = right - wrong
            outer, inner = gap[0:1], gap[1:2]
            fix = jnp.where(row == 7, second * outer + last * inner, 0.0)
            fix = fix + jnp.where(row == 6, last * outer, 0.0)
            conv[target + BLOCK - 8 : target + BLOCK] += fix
        else:
            right = masked[pl.ds(start, 16)].astype(F32)
            wrong = masked[pl.ds(pl.multiple_of(start + SPAN, 16), 16)].astype(F32)
            gap = right - wrong
            outer, inner = gap[15:16], gap[14:15]
            fix = jnp.where(row == 0, second * outer + last * inner, 0.0)
            fix = fix + jnp.where(row == 1, last * outer, 0.0)
            conv[target : target + 8] += fix

    complete(1)

    def store(tile):
        rows = pl.ds(pl.multiple_of(tile * 2 * TILE, TILE), 2 * TILE)
        return pltpu.make_async_copy(normed.at[rows], gated_out.at[rows], store_sem.at[tile])

    def gate_pass(tile, carry):
        start = pl.multiple_of(tile * TILE, TILE)
        rows = pl.ds(pl.multiple_of(tile * 2 * TILE, TILE), 2 * TILE)
        for strand in range(2):
            for offset in range(0, TILE, BLOCK):
                filtered(strand, pl.multiple_of(start + offset, BLOCK), strand * TILE + offset)
        half_gate = 0.5 * dot(normed[rows], weights[1])
        gated = (half_gate * jnp.tanh(half_gate) + half_gate) * conv[...]
        normed[rows] = gated.astype(BF16)
        store(tile).start()
        return carry

    lax.fori_loop(0, ROWS // TILE, gate_pass, 0)
    complete(2)
    last_store = pltpu.make_async_copy(weights.at[2], last_weights, store_sem.at[ROWS // TILE])
    last_store.start()

    for copy in halos:
        copy.wait_send()
    for part in range(3):
        z_owner(part, sent)
        ring_owner(part, sent)

        @pl.when(fetches == 1)
        def _(part=part):
            for copy in ring_copies(part):
                copy.wait_send()
            aside(part, y, 0).wait_send()
            to_mate(part, y, 0).wait_send()

        for index, row in enumerate((below, above, across)):
            aside(part, row, index + 1).wait_send()
            to_mate(part, row, index + 1).wait_send()
    for tile in range(ROWS // TILE):
        store(tile).wait()
    last_store.wait()


def finish_kernel(
    hidden, gated_source, weight_source, out, weight, gated, state, load_sem, ready_sem, store_sem
):
    def fetch(unit):
        rows = pl.ds(pl.multiple_of(unit * PART, PART), PART)
        own = pl.multiple_of(unit * 2 * PART, PART)
        loads = [pltpu.make_async_copy(hidden.at[rows], state.at[rows], ready_sem.at[unit])]
        for strand in range(2):
            start = unit // 2 * (2 * TILE) + strand * TILE + unit % 2 * PART
            loads.append(
                pltpu.make_async_copy(
                    gated_source.at[pl.ds(pl.multiple_of(start, PART), PART)],
                    gated.at[pl.ds(own + strand * PART, PART)],
                    load_sem.at[unit, strand],
                )
            )
        return *loads, pltpu.make_async_copy(state.at[rows], out.at[rows], store_sem.at[unit])

    units = ROWS // PART
    first = pltpu.make_async_copy(weight_source, weight, load_sem.at[units, 0])
    first.start()
    for unit in range(units):
        for copy in fetch(unit)[:-1]:
            copy.start()
    first.wait()

    def out_pass(unit, carry):
        rows = pl.ds(pl.multiple_of(unit * PART, PART), PART)
        own = pl.ds(pl.multiple_of(unit * 2 * PART, PART), 2 * PART)
        *loads, store = fetch(unit)
        for copy in loads:
            copy.wait()
        branch = jnp.dot(gated[own], weight[...], preferred_element_type=F32)
        for strand in range(2):
            columns = slice(strand * WIDTH, strand * WIDTH + WIDTH)
            added = branch[strand * PART : strand * PART + PART]
            state[rows, columns] = (state[rows, columns].astype(F32) + added).astype(BF16)
        store.start()
        return carry

    lax.fori_loop(0, units, out_pass, 0)
    for unit in range(units):
        fetch(unit)[-1].wait()


def shards(
    hidden_state, tokens, in_codes, in_scales, out_codes, out_scales, short_filter, long_filter
):
    window = hidden_state[0]
    anywhere = pl.BlockSpec(memory_space=pl.ANY)
    dma = pltpu.SemaphoreType.DMA
    tables = constants()
    gated, last_weights = pl.pallas_call(
        layer_kernel,
        out_shape=(
            jax.ShapeDtypeStruct((2 * ROWS, WIDTH), BF16),
            jax.ShapeDtypeStruct((WIDTH, WIDTH), BF16),
        ),
        in_specs=[anywhere] * (8 + len(tables)),
        out_specs=(anywhere, anywhere),
        scratch_shapes=[
            pltpu.VMEM((3, WIDTH, WIDTH), BF16),
            pltpu.VMEM((3, 32, 2 * WIDTH), BF16),
            pltpu.VMEM((3, 32, WIDTH), BF16),
            pltpu.VMEM((3, 12), F32),
            pltpu.VMEM((3, 6), F32),
            pltpu.VMEM((1, ROWS), jnp.int32),
            pltpu.VMEM((1, 256), jnp.int32),
            pltpu.VMEM((1, 256), jnp.int32),
            pltpu.VMEM((HALO, WIDTH), BF16),
            pltpu.VMEM((HALO, WIDTH), BF16),
            pltpu.VMEM((SHORT, WIDTH), BF16),
            pltpu.VMEM((LONG, WIDTH), BF16),
            *(pltpu.VMEM(table.shape, BF16) for table in tables),
            pltpu.VMEM((2, ROWS, WIDTH), BF16),
            pltpu.VMEM((2 * ROWS + 2 * HALO, WIDTH), BF16),
            pltpu.VMEM((ROWS + HALO, WIDTH), BF16),
            pltpu.VMEM((ROWS + HALO, WIDTH), BF16),
            pltpu.VMEM((ROWS + 512, 128), F32),
            pltpu.VMEM((BLOCK, WIDTH), F32),
            pltpu.VMEM((BLOCK, WIDTH), F32),
            pltpu.VMEM((BLOCK, WIDTH), F32),
            pltpu.VMEM((8, WIDTH), F32),
            pltpu.VMEM((2 * TILE, WIDTH), F32),
            dma((16,)),
            dma((8,)),
            dma((3, 4)),
            dma((3, 4)),
            dma((3, 4)),
            dma((4,)),
            dma((3, 2)),
            dma((3, 3)),
            dma((3, 4)),
            dma((3, 4)),
            dma((4,)),
        ],
        compiler_params=pltpu.CompilerParams(
            collective_id=0, has_side_effects=True, vmem_limit_bytes=VMEM_LIMIT
        ),
        name="layer",
    )(
        window,
        tokens,
        in_codes,
        in_scales,
        out_codes,
        out_scales,
        short_filter,
        long_filter,
        *map(jnp.asarray, tables),
    )
    result = pl.pallas_call(
        finish_kernel,
        out_shape=jax.ShapeDtypeStruct((ROWS, 2 * WIDTH), BF16),
        in_specs=[anywhere] * 3,
        out_specs=anywhere,
        scratch_shapes=[
            pltpu.VMEM((WIDTH, WIDTH), BF16),
            pltpu.VMEM((2 * ROWS, WIDTH), BF16),
            pltpu.VMEM((ROWS, 2 * WIDTH), BF16),
            dma((ROWS // PART + 1, 2)),
            dma((8,)),
            dma((8,)),
        ],
        compiler_params=pltpu.CompilerParams(vmem_limit_bytes=VMEM_LIMIT),
        name="finish",
    )(window, gated, last_weights)
    return result[None]


def solution(mesh):
    in_specs = (
        P("dp", "ctx", None),
        P("dp", "ctx"),
        P("dp", None, None),
        P("dp", None),
        P("dp", None, None),
        P("dp", None),
        P(),
        P(),
    )
    out_specs = P("dp", "ctx", None)
    return jax.shard_map(shards, mesh=mesh, in_specs=in_specs, out_specs=out_specs, check_vma=False)
```

```python
import functools

import jax
import jax.numpy as jnp
import numpy as np
from jax import lax
from jax.experimental import pallas as pl
from jax.experimental.pallas import tpu as pltpu
from jax.sharding import PartitionSpec as P

MESH = pl.DeviceIdType.MESH
F32, BF16 = jnp.float32, jnp.bfloat16
ROWS, HALO = 1024, 144
WIDTH, SHARD = 768, 96
BLOCK, SPAN = 128, 256
TILE, PART = 512, 256
DP, CTX = 8, 32
LONG, SHORT = 128, 4
VMEM_LIMIT = 63 << 20


def transform(positions):
    freq = np.arange(BLOCK)[:, None]
    angle = 2 * np.pi * ((freq * positions[None, :]) % SPAN) / SPAN
    real, imag = np.cos(angle), -np.sin(angle)
    imag[0] = np.cos(np.pi * (positions % 2))
    return np.concatenate([real, imag], axis=0)


def split(matrix):
    high = matrix.astype(np.float32).astype(BF16)
    return high, (matrix - high.astype(np.float64)).astype(np.float32).astype(BF16)


def constants():
    spread = transform(np.arange(SPAN))
    long_high, long_low = split(transform(LONG - 1 - np.arange(LONG)))
    short_table = np.zeros((SPAN, 16))
    short_table[:, :SHORT] = transform(SHORT - 1 - np.arange(SHORT))
    short_high, short_low = split(short_table)
    as_bf16 = lambda table: table.astype(np.float32).astype(BF16)
    gather_forward = as_bf16(spread[:, BLOCK:].T)
    gather_backward = as_bf16(spread[:, :BLOCK].T)
    return (
        as_bf16(spread),
        gather_forward,
        gather_backward,
        long_high,
        long_low,
        short_high,
        short_low,
    )


def layer_kernel(
    hidden,
    tokens,
    in_codes,
    in_scales,
    out_codes,
    out_scales,
    short_source,
    long_source,
    spread_source,
    gather_forward_source,
    gather_backward_source,
    long_high_source,
    long_low_source,
    short_high_source,
    short_low_source,
    gated_out,
    last_weights,
    weights,
    codes,
    last_codes,
    scales,
    last_scales,
    letters,
    token_forward,
    token_backward,
    halo_forward,
    halo_backward,
    short_filter,
    long_filter,
    spread,
    gather_forward,
    gather_backward,
    long_high,
    long_low,
    short_high,
    short_low,
    state,
    normed,
    masked_forward,
    masked_backward,
    keep,
    pure,
    cross,
    edge,
    taps,
    conv,
    load_sem,
    store_sem,
    piece_recv,
    cross_recv,
    mate_recv,
    halo_recv,
    z_send,
    y_send,
    x_send,
    mate_send,
    halo_send,
):
    dp, ctx = lax.axis_index("dp"), lax.axis_index("ctx")
    y, z_high = dp // 2, dp % 2
    z_low, x, core = ctx // 8, (ctx // 2) % 4, ctx % 2
    half = x % 2
    partner = dp + 1 - 2 * z_high
    ring = 4
    below, above, across = (y + 3) % ring, (y + 1) % ring, (y + 2) % ring
    up, down = ((dp + 2) % DP, ctx), ((dp + DP - 2) % DP, ctx)
    opposite = ((dp + 4) % DP, ctx)
    step = 1 - 2 * core

    def along_x(distance):
        return (dp, z_low * 8 + (x + ring + distance) % ring * 2 + core)

    beside = along_x(step)
    mate = (dp, ctx + step)
    after, before = (dp, (ctx + 1) % CTX), (dp, (ctx + CTX - 1) % CTX)
    border = z_low // 3 + (3 - z_low) // 3
    fetches = (core + z_high) % 2

    barrier = pltpu.get_barrier_semaphore()
    for device in (up, down, opposite, along_x(-step), mate, after, before):
        pl.semaphore_signal(barrier, inc=1, device_id=device, device_id_type=MESH)

    @pl.when(fetches == 1)
    def _():
        shift = (z_low // 2) * 24
        source = (partner, ctx + 24 - 8 * z_low - shift)
        pl.semaphore_signal(barrier, inc=1, device_id=source, device_id_type=MESH)

    loads = []

    def load(source, target):
        index = len(loads)
        copy = pltpu.make_async_copy(source, target, load_sem.at[index])
        copy.start()
        loads.append(copy)
        return copy

    code_loads = [load(in_codes, codes), load(in_scales, scales)]
    last_loads = [load(out_codes, last_codes), load(out_scales, last_scales)]
    letter_load = load(tokens, letters)
    filter_loads = [
        load(short_source, short_filter),
        load(long_source, long_filter),
        load(long_high_source, long_high),
        load(long_low_source, long_low),
        load(short_high_source, short_high),
        load(short_low_source, short_low),
    ]
    state_loads = [
        load(hidden.at[:, pl.ds(strand * WIDTH, WIDTH)], state.at[strand]) for strand in range(2)
    ]
    table_loads = [
        load(spread_source, spread),
        load(gather_forward_source, gather_forward),
        load(gather_backward_source, gather_backward),
    ]

    def base_of(row, side):
        return (2 * row + side) * SHARD

    def dequantise(part):
        for block in range(3):
            start = base_of(y, z_high) + block * 32
            rows = pl.ds(pl.multiple_of(start, 32), 32)
            for group in range(6):
                column = group * 128
                if part < 2:
                    place = part * 6 + group
                    values = codes[block, :, place * 128 : place * 128 + 128]
                    scale = scales[block : block + 1, place : place + 1]
                else:
                    values = last_codes[block, :, column : column + 128]
                    scale = last_scales[block : block + 1, group : group + 1]
                weights[part, rows, column : column + 128] = (values.astype(F32) * scale).astype(BF16)

    for copy in code_loads:
        copy.wait()
    dequantise(0)
    pl.semaphore_wait(barrier, 7 + 2 * border * (1 - fetches))

    def piece(part, row, side):
        start = base_of(row, core) + side * (SHARD // 2)
        return weights.at[part, pl.ds(pl.multiple_of(start, 16), SHARD // 2)]

    def remote(ref, device, left, received):
        return pltpu.make_async_remote_copy(
            src_ref=ref,
            dst_ref=ref,
            send_sem=left,
            recv_sem=received,
            device_id=device,
            device_id_type=MESH,
        )

    def along(part, row, device, index):
        return remote(
            piece(part, row, half), device, y_send.at[part, index], piece_recv.at[part, row]
        )

    def aside(part, row, index):
        return remote(
            piece(part, row, half),
            beside,
            x_send.at[part, index],
            cross_recv.at[part, row],
        )

    def to_mate(part, row, index):
        ref = weights.at[part, pl.ds(pl.multiple_of(base_of(row, core), 32), SHARD)]
        return remote(ref, mate, mate_send.at[part, index], mate_recv.at[part, row])

    def z_copies(part):
        sign = 1 - 2 * (z_low // 3)
        return [
            remote(
                piece(part, y, half),
                (partner, ctx + distance * sign),
                z_send.at[part, index],
                piece_recv.at[part, y],
            )
            for index, distance in enumerate((24, 16))
        ]

    def ring_copies(part):
        return [along(part, y, up, 0), along(part, y, down, 1), along(part, y, opposite, 2)]

    def z_owner(part, action):
        @pl.when(fetches + (1 - border) == 0)
        def _():
            for copy in z_copies(part):
                action(copy)

    def ring_owner(part, action):
        @pl.when(fetches == 0)
        def _():
            for copy in ring_copies(part):
                action(copy)

    def start(copy):
        copy.start()

    def sent(copy):
        copy.wait_send()

    def relay(part):
        @pl.when(fetches == 1)
        def _():
            along(part, y, up, 0).wait_recv()
            for copy in ring_copies(part):
                copy.start()
            aside(part, y, 0).start()

    def collect(part):
        for index, row in enumerate((below, above, across)):
            along(part, row, up, 0).wait_recv()
            aside(part, row, index + 1).start()

    def share(part):
        def pass_on(row, index):
            remote(
                piece(part, row, 1 - half), beside, x_send.at[part, 0], cross_recv.at[part, row]
            ).wait_recv()
            to_mate(part, row, index).start()

        @pl.when(fetches == 1)
        def _():
            pass_on(y, 0)

        for index, row in enumerate((below, above, across)):
            pass_on(row, index + 1)

    def complete(part):
        def finish(row):
            ref = weights.at[part, pl.ds(pl.multiple_of(base_of(row, 1 - core), 32), SHARD)]
            remote(ref, mate, mate_send.at[part, 0], mate_recv.at[part, row]).wait_recv()

        @pl.when(fetches == 0)
        def _():
            finish(y)

        for row in (below, above, across):
            finish(row)

    halos = []

    def halo(source, target, device):
        index = len(halos)
        copy = pltpu.make_async_remote_copy(
            src_ref=source,
            dst_ref=target,
            send_sem=halo_send.at[index],
            recv_sem=halo_recv.at[index],
            device_id=device,
            device_id_type=MESH,
        )
        copy.start()
        halos.append(copy)

    def open_part(part):
        z_owner(part, start)
        ring_owner(part, start)

    open_part(0)
    for copy in last_loads:
        copy.wait()
    dequantise(1)
    open_part(1)
    dequantise(2)
    open_part(2)
    letter_load.wait()
    halo(letters.at[:, pl.ds(ROWS - 256, 256)], token_forward, after)
    halo(letters.at[:, pl.ds(0, 256)], token_backward, before)
    halo(hidden.at[pl.ds(ROWS - HALO, HALO), pl.ds(0, WIDTH)], halo_forward, after)
    halo(hidden.at[pl.ds(0, HALO), pl.ds(WIDTH, WIDTH)], halo_backward, before)

    def keep_rows(values, live):
        flags = jnp.where(values != 4, live, 0.0)
        return jnp.transpose(jnp.broadcast_to(flags, (128, 128)))

    one = jnp.float32(1.0)
    for block in range(ROWS // 128):
        keep[block * 128 + 256 : block * 128 + 384] = keep_rows(
            letters[:, block * 128 : block * 128 + 128], one
        )

    def project(values):
        wide = values.astype(F32)
        mean = jnp.mean(wide * wide, axis=-1, keepdims=True)
        return (wide * lax.rsqrt(mean + 1e-5)).astype(BF16)

    def norm_pass(part, carry):
        rows = pl.ds(pl.multiple_of(part * PART, PART), PART)
        for strand in range(2):
            start = part // 2 * (2 * TILE) + strand * TILE + part % 2 * PART
            normed[pl.ds(pl.multiple_of(start, PART), PART)] = project(state[strand, rows])
        return carry

    for copy in state_loads:
        copy.wait()
    lax.fori_loop(0, 1, norm_pass, 0)
    relay(0)
    lax.fori_loop(1, 3, norm_pass, 0)
    relay(1)
    lax.fori_loop(3, 4, norm_pass, 0)
    collect(0)
    relay(2)
    collect(1)

    for copy in filter_loads:
        copy.wait()
    short = short_filter[...].astype(F32)
    long = long_filter[...]
    padded = jnp.concatenate([short, jnp.zeros((16 - SHORT, WIDTH), F32)], axis=0).astype(BF16)
    dot = functools.partial(jnp.dot, preferred_element_type=F32)
    long_hat = dot(long_high[...], long) + dot(long_low[...], long)
    short_hat = dot(short_high[...], padded) + dot(short_low[...], padded)
    real_long, imag_long = long_hat[:BLOCK], long_hat[BLOCK:]
    real_short, imag_short = short_hat[:BLOCK], short_hat[BLOCK:]
    first = lax.broadcasted_iota(jnp.int32, (BLOCK, WIDTH), 0) == 0
    scale = jnp.where(first, 1.0 / SPAN, 2.0 / SPAN)
    reals, imags = real_short * real_long, imag_short * imag_long
    pure[...] = jnp.where(first, reals, reals - imags) * scale
    edge[...] = jnp.where(first, imags, reals - imags) * scale
    cross[...] = jnp.where(first, 0.0, real_short * imag_long + imag_short * real_long) * scale
    long_head = long[:16].astype(F32)
    taps[0:1] = short[0:1] * long_head[0:1]
    taps[1:2] = short[0:1] * long_head[1:2] + short[1:2] * long_head[0:1]

    for copy in table_loads:
        copy.wait()
    share(0)
    complete(0)

    def value_tile(tile, count):
        start = tile * TILE
        values = dot(normed[2 * start : 2 * start + count], weights[0])
        flags = jnp.tile(keep[start + 256 : start + 256 + TILE], (1, 6))
        masked_forward[start + HALO : start + HALO + TILE] = (values[:TILE] * flags).astype(BF16)
        masked_backward[start : start + TILE] = (values[TILE : 2 * TILE] * flags).astype(BF16)
        return values[2 * TILE :]

    value_tile(0, 2 * TILE)
    collect(2)
    share(1)
    for copy in halos:
        copy.wait_recv()
    live_before = jnp.where(ctx > 0, 1.0, 0.0)
    live_after = jnp.where(ctx < CTX - 1, 1.0, 0.0)
    for block in range(2):
        columns = slice(block * 128, block * 128 + 128)
        keep[columns] = keep_rows(token_forward[:, columns], live_before)
        keep[ROWS + 256 + block * 128 : ROWS + 384 + block * 128] = keep_rows(
            token_backward[:, columns], live_after
        )
    normed[2 * ROWS : 2 * ROWS + HALO] = project(halo_forward[...])
    normed[2 * ROWS + HALO :] = project(halo_backward[...])
    rims = value_tile(1, 2 * TILE + 2 * HALO)
    masked_forward[:HALO] = (rims[:HALO] * jnp.tile(keep[256 - HALO : 256], (1, 6))).astype(BF16)
    masked_backward[ROWS:] = (
        rims[HALO:] * jnp.tile(keep[ROWS + 256 : ROWS + 256 + HALO], (1, 6))
    ).astype(BF16)

    def filtered(strand, start, target):
        masked = masked_backward if strand else masked_forward
        origin = start if strand else pl.multiple_of(start + 16, 16)
        window = masked[pl.ds(origin, SPAN)]
        waves = dot(spread[...], window)
        real, imag = waves[:BLOCK], waves[BLOCK:]
        straight, turned = real * pure[...], imag * cross[...]
        upright, bent = imag * edge[...], real * cross[...]
        if strand:
            parts = [straight + turned, upright - bent]
        else:
            parts = [straight - turned, upright + bent]
        product = jnp.concatenate([part.astype(BF16) for part in parts], axis=0)
        gather = gather_backward if strand else gather_forward
        conv[target : target + BLOCK] = dot(gather[...], product)
        last, second = taps[0:1], taps[1:2]
        row = lax.broadcasted_iota(jnp.int32, (8, WIDTH), 0)
        if strand:
            wrong = masked[pl.ds(start, 16)].astype(F32)
            right = masked[pl.ds(pl.multiple_of(start + SPAN, 16), 16)].astype(F32)
            gap = right - wrong
            outer, inner = gap[0:1], gap[1:2]
            fix = jnp.where(row == 7, second * outer + last * inner, 0.0)
            fix = fix + jnp.where(row == 6, last * outer, 0.0)
            conv[target + BLOCK - 8 : target + BLOCK] += fix
        else:
            right = masked[pl.ds(start, 16)].astype(F32)
            wrong = masked[pl.ds(pl.multiple_of(start + SPAN, 16), 16)].astype(F32)
            gap = right - wrong
            outer, inner = gap[15:16], gap[14:15]
            fix = jnp.where(row == 0, second * outer + last * inner, 0.0)
            fix = fix + jnp.where(row == 1, last * outer, 0.0)
            conv[target : target + 8] += fix

    complete(1)

    def store(tile):
        rows = pl.ds(pl.multiple_of(tile * 2 * TILE, TILE), 2 * TILE)
        return pltpu.make_async_copy(normed.at[rows], gated_out.at[rows], store_sem.at[tile])

    def gate_pass(tile, carry):
        start = pl.multiple_of(tile * TILE, TILE)
        rows = pl.ds(pl.multiple_of(tile * 2 * TILE, TILE), 2 * TILE)
        for strand in range(2):
            for offset in range(0, TILE, BLOCK):
                filtered(strand, pl.multiple_of(start + offset, BLOCK), strand * TILE + offset)
        half_gate = 0.5 * dot(normed[rows], weights[1])
        gated = (half_gate * jnp.tanh(half_gate) + half_gate) * conv[...]
        normed[rows] = gated.astype(BF16)
        store(tile).start()
        return carry

    lax.fori_loop(0, 1, gate_pass, 0)
    share(2)
    lax.fori_loop(1, ROWS // TILE, gate_pass, 0)
    complete(2)
    last_store = pltpu.make_async_copy(weights.at[2], last_weights, store_sem.at[ROWS // TILE])
    last_store.start()

    for copy in halos:
        copy.wait_send()
    for part in range(3):
        z_owner(part, sent)
        ring_owner(part, sent)

        @pl.when(fetches == 1)
        def _(part=part):
            for copy in ring_copies(part):
                copy.wait_send()
            aside(part, y, 0).wait_send()
            to_mate(part, y, 0).wait_send()

        for index, row in enumerate((below, above, across)):
            aside(part, row, index + 1).wait_send()
            to_mate(part, row, index + 1).wait_send()
    for tile in range(ROWS // TILE):
        store(tile).wait()
    last_store.wait()


def finish_kernel(
    hidden, gated_source, weight_source, out, weight, gated, state, load_sem, ready_sem, store_sem
):
    def fetch(unit):
        rows = pl.ds(pl.multiple_of(unit * PART, PART), PART)
        own = pl.multiple_of(unit * 2 * PART, PART)
        loads = [pltpu.make_async_copy(hidden.at[rows], state.at[rows], ready_sem.at[unit])]
        for strand in range(2):
            start = unit // 2 * (2 * TILE) + strand * TILE + unit % 2 * PART
            loads.append(
                pltpu.make_async_copy(
                    gated_source.at[pl.ds(pl.multiple_of(start, PART), PART)],
                    gated.at[pl.ds(own + strand * PART, PART)],
                    load_sem.at[unit, strand],
                )
            )
        return *loads, pltpu.make_async_copy(state.at[rows], out.at[rows], store_sem.at[unit])

    units = ROWS // PART
    first = pltpu.make_async_copy(weight_source, weight, load_sem.at[units, 0])
    first.start()
    for unit in range(units):
        for copy in fetch(unit)[:-1]:
            copy.start()
    first.wait()

    def out_pass(unit, carry):
        rows = pl.ds(pl.multiple_of(unit * PART, PART), PART)
        own = pl.ds(pl.multiple_of(unit * 2 * PART, PART), 2 * PART)
        *loads, store = fetch(unit)
        for copy in loads:
            copy.wait()
        branch = jnp.dot(gated[own], weight[...], preferred_element_type=F32)
        for strand in range(2):
            columns = slice(strand * WIDTH, strand * WIDTH + WIDTH)
            added = branch[strand * PART : strand * PART + PART]
            state[rows, columns] = (state[rows, columns].astype(F32) + added).astype(BF16)
        store.start()
        return carry

    lax.fori_loop(0, units, out_pass, 0)
    for unit in range(units):
        fetch(unit)[-1].wait()


def shards(
    hidden_state, tokens, in_codes, in_scales, out_codes, out_scales, short_filter, long_filter
):
    window = hidden_state[0]
    anywhere = pl.BlockSpec(memory_space=pl.ANY)
    dma = pltpu.SemaphoreType.DMA
    tables = constants()
    gated, last_weights = pl.pallas_call(
        layer_kernel,
        out_shape=(
            jax.ShapeDtypeStruct((2 * ROWS, WIDTH), BF16),
            jax.ShapeDtypeStruct((WIDTH, WIDTH), BF16),
        ),
        in_specs=[anywhere] * (8 + len(tables)),
        out_specs=(anywhere, anywhere),
        scratch_shapes=[
            pltpu.VMEM((3, WIDTH, WIDTH), BF16),
            pltpu.VMEM((3, 32, 2 * WIDTH), BF16),
            pltpu.VMEM((3, 32, WIDTH), BF16),
            pltpu.VMEM((3, 12), F32),
            pltpu.VMEM((3, 6), F32),
            pltpu.VMEM((1, ROWS), jnp.int32),
            pltpu.VMEM((1, 256), jnp.int32),
            pltpu.VMEM((1, 256), jnp.int32),
            pltpu.VMEM((HALO, WIDTH), BF16),
            pltpu.VMEM((HALO, WIDTH), BF16),
            pltpu.VMEM((SHORT, WIDTH), BF16),
            pltpu.VMEM((LONG, WIDTH), BF16),
            *(pltpu.VMEM(table.shape, BF16) for table in tables),
            pltpu.VMEM((2, ROWS, WIDTH), BF16),
            pltpu.VMEM((2 * ROWS + 2 * HALO, WIDTH), BF16),
            pltpu.VMEM((ROWS + HALO, WIDTH), BF16),
            pltpu.VMEM((ROWS + HALO, WIDTH), BF16),
            pltpu.VMEM((ROWS + 512, 128), F32),
            pltpu.VMEM((BLOCK, WIDTH), F32),
            pltpu.VMEM((BLOCK, WIDTH), F32),
            pltpu.VMEM((BLOCK, WIDTH), F32),
            pltpu.VMEM((8, WIDTH), F32),
            pltpu.VMEM((2 * TILE, WIDTH), F32),
            dma((16,)),
            dma((8,)),
            dma((3, 4)),
            dma((3, 4)),
            dma((3, 4)),
            dma((4,)),
            dma((3, 2)),
            dma((3, 3)),
            dma((3, 4)),
            dma((3, 4)),
            dma((4,)),
        ],
        compiler_params=pltpu.CompilerParams(
            collective_id=0, has_side_effects=True, vmem_limit_bytes=VMEM_LIMIT
        ),
        name="layer",
    )(
        window,
        tokens,
        in_codes,
        in_scales,
        out_codes,
        out_scales,
        short_filter,
        long_filter,
        *map(jnp.asarray, tables),
    )
    result = pl.pallas_call(
        finish_kernel,
        out_shape=jax.ShapeDtypeStruct((ROWS, 2 * WIDTH), BF16),
        in_specs=[anywhere] * 3,
        out_specs=anywhere,
        scratch_shapes=[
            pltpu.VMEM((WIDTH, WIDTH), BF16),
            pltpu.VMEM((2 * ROWS, WIDTH), BF16),
            pltpu.VMEM((ROWS, 2 * WIDTH), BF16),
            dma((ROWS // PART + 1, 2)),
            dma((8,)),
            dma((8,)),
        ],
        compiler_params=pltpu.CompilerParams(vmem_limit_bytes=VMEM_LIMIT),
        name="finish",
    )(window, gated, last_weights)
    return result[None]


def solution(mesh):
    in_specs = (
        P("dp", "ctx", None),
        P("dp", "ctx"),
        P("dp", None, None),
        P("dp", None),
        P("dp", None, None),
        P("dp", None),
        P(),
        P(),
    )
    out_specs = P("dp", "ctx", None)
    return jax.shard_map(shards, mesh=mesh, in_specs=in_specs, out_specs=out_specs, check_vma=False)
```

```python
import functools

import jax
import jax.numpy as jnp
import numpy as np
from jax import lax
from jax.experimental import pallas as pl
from jax.experimental.pallas import tpu as pltpu
from jax.sharding import PartitionSpec as P

MESH = pl.DeviceIdType.MESH
F32, BF16 = jnp.float32, jnp.bfloat16
ROWS, HALO = 1024, 144
WIDTH, SHARD = 768, 96
BLOCK, SPAN = 128, 256
TILE, PART = 512, 256
DP, CTX = 8, 32
LONG, SHORT = 128, 4
VMEM_LIMIT = 63 << 20


def transform(positions):
    freq = np.arange(BLOCK)[:, None]
    angle = 2 * np.pi * ((freq * positions[None, :]) % SPAN) / SPAN
    real, imag = np.cos(angle), -np.sin(angle)
    imag[0] = np.cos(np.pi * (positions % 2))
    return np.concatenate([real, imag], axis=0)


def split(matrix):
    high = matrix.astype(np.float32).astype(BF16)
    return high, (matrix - high.astype(np.float64)).astype(np.float32).astype(BF16)


def constants():
    spread = transform(np.arange(SPAN))
    long_high, long_low = split(transform(LONG - 1 - np.arange(LONG)))
    short_table = np.zeros((SPAN, 16))
    short_table[:, :SHORT] = transform(SHORT - 1 - np.arange(SHORT))
    short_high, short_low = split(short_table)
    as_bf16 = lambda table: table.astype(np.float32).astype(BF16)
    gather_forward = as_bf16(spread[:, BLOCK:].T)
    gather_backward = as_bf16(spread[:, :BLOCK].T)
    return (
        as_bf16(spread),
        gather_forward,
        gather_backward,
        long_high,
        long_low,
        short_high,
        short_low,
    )


def layer_kernel(
    hidden,
    tokens,
    in_codes,
    in_scales,
    out_codes,
    out_scales,
    short_source,
    long_source,
    spread_source,
    gather_forward_source,
    gather_backward_source,
    long_high_source,
    long_low_source,
    short_high_source,
    short_low_source,
    gated_out,
    last_weights,
    weights,
    codes,
    last_codes,
    scales,
    last_scales,
    letters,
    token_forward,
    token_backward,
    halo_forward,
    halo_backward,
    short_filter,
    long_filter,
    spread,
    gather_forward,
    gather_backward,
    long_high,
    long_low,
    short_high,
    short_low,
    state,
    normed,
    masked_forward,
    masked_backward,
    keep,
    pure,
    cross,
    edge,
    taps,
    conv,
    load_sem,
    store_sem,
    piece_recv,
    cross_recv,
    mate_recv,
    halo_recv,
    z_send,
    y_send,
    x_send,
    mate_send,
    halo_send,
):
    dp, ctx = lax.axis_index("dp"), lax.axis_index("ctx")
    y, z_high = dp // 2, dp % 2
    z_low, x, core = ctx // 8, (ctx // 2) % 4, ctx % 2
    half = x % 2
    partner = dp + 1 - 2 * z_high
    ring = 4
    below, above, across = (y + 3) % ring, (y + 1) % ring, (y + 2) % ring
    up, down = ((dp + 2) % DP, ctx), ((dp + DP - 2) % DP, ctx)
    opposite = ((dp + 4) % DP, ctx)
    step = 1 - 2 * core

    def along_x(distance):
        return (dp, z_low * 8 + (x + ring + distance) % ring * 2 + core)

    beside = along_x(step)
    mate = (dp, ctx + step)
    after, before = (dp, (ctx + 1) % CTX), (dp, (ctx + CTX - 1) % CTX)
    border = z_low // 3 + (3 - z_low) // 3
    fetches = (core + z_high) % 2

    barrier = pltpu.get_barrier_semaphore()
    for device in (up, down, opposite, along_x(-step), mate, after, before):
        pl.semaphore_signal(barrier, inc=1, device_id=device, device_id_type=MESH)

    @pl.when(fetches == 1)
    def _():
        shift = (z_low // 2) * 24
        source = (partner, ctx + 24 - 8 * z_low - shift)
        pl.semaphore_signal(barrier, inc=1, device_id=source, device_id_type=MESH)

    loads = []

    def load(source, target):
        index = len(loads)
        copy = pltpu.make_async_copy(source, target, load_sem.at[index])
        copy.start()
        loads.append(copy)
        return copy

    code_loads = [load(in_codes, codes), load(in_scales, scales)]
    last_loads = [load(out_codes, last_codes), load(out_scales, last_scales)]
    letter_load = load(tokens, letters)
    filter_loads = [
        load(short_source, short_filter),
        load(long_source, long_filter),
        load(long_high_source, long_high),
        load(long_low_source, long_low),
        load(short_high_source, short_high),
        load(short_low_source, short_low),
    ]
    state_loads = [
        load(hidden.at[:, pl.ds(strand * WIDTH, WIDTH)], state.at[strand]) for strand in range(2)
    ]
    table_loads = [
        load(spread_source, spread),
        load(gather_forward_source, gather_forward),
        load(gather_backward_source, gather_backward),
    ]

    def base_of(row, side):
        return (2 * row + side) * SHARD

    def dequantise(part):
        for block in range(3):
            start = base_of(y, z_high) + block * 32
            rows = pl.ds(pl.multiple_of(start, 32), 32)
            for group in range(6):
                column = group * 128
                if part < 2:
                    place = part * 6 + group
                    values = codes[block, :, place * 128 : place * 128 + 128]
                    scale = scales[block : block + 1, place : place + 1]
                else:
                    values = last_codes[block, :, column : column + 128]
                    scale = last_scales[block : block + 1, group : group + 1]
                weights[part, rows, column : column + 128] = (values.astype(F32) * scale).astype(BF16)

    for copy in code_loads:
        copy.wait()
    dequantise(0)
    pl.semaphore_wait(barrier, 7 + 2 * border * (1 - fetches))

    def piece(part, row, side):
        start = base_of(row, core) + side * (SHARD // 2)
        return weights.at[part, pl.ds(pl.multiple_of(start, 16), SHARD // 2)]

    def remote(ref, device, left, received):
        return pltpu.make_async_remote_copy(
            src_ref=ref,
            dst_ref=ref,
            send_sem=left,
            recv_sem=received,
            device_id=device,
            device_id_type=MESH,
        )

    def along(part, row, device, index):
        return remote(
            piece(part, row, half), device, y_send.at[part, index], piece_recv.at[part, row]
        )

    def aside(part, row, index):
        return remote(
            piece(part, row, half),
            beside,
            x_send.at[part, index],
            cross_recv.at[part, row],
        )

    def to_mate(part, row, index):
        ref = weights.at[part, pl.ds(pl.multiple_of(base_of(row, core), 32), SHARD)]
        return remote(ref, mate, mate_send.at[part, index], mate_recv.at[part, row])

    def z_copies(part):
        sign = 1 - 2 * (z_low // 3)
        return [
            remote(
                piece(part, y, half),
                (partner, ctx + distance * sign),
                z_send.at[part, index],
                piece_recv.at[part, y],
            )
            for index, distance in enumerate((24, 16))
        ]

    def ring_copies(part):
        return [along(part, y, up, 0), along(part, y, down, 1), along(part, y, opposite, 2)]

    def z_owner(part, action):
        @pl.when(fetches + (1 - border) == 0)
        def _():
            for copy in z_copies(part):
                action(copy)

    def ring_owner(part, action):
        @pl.when(fetches == 0)
        def _():
            for copy in ring_copies(part):
                action(copy)

    def start(copy):
        copy.start()

    def sent(copy):
        copy.wait_send()

    def relay(part):
        @pl.when(fetches == 1)
        def _():
            along(part, y, up, 0).wait_recv()
            for copy in ring_copies(part):
                copy.start()
            aside(part, y, 0).start()

    def collect(part):
        for index, row in enumerate((below, above, across)):
            along(part, row, up, 0).wait_recv()
            aside(part, row, index + 1).start()

    def share(part):
        def pass_on(row, index):
            remote(
                piece(part, row, 1 - half), beside, x_send.at[part, 0], cross_recv.at[part, row]
            ).wait_recv()
            to_mate(part, row, index).start()

        @pl.when(fetches == 1)
        def _():
            pass_on(y, 0)

        for index, row in enumerate((below, above, across)):
            pass_on(row, index + 1)

    def complete(part):
        def finish(row):
            ref = weights.at[part, pl.ds(pl.multiple_of(base_of(row, 1 - core), 32), SHARD)]
            remote(ref, mate, mate_send.at[part, 0], mate_recv.at[part, row]).wait_recv()

        @pl.when(fetches == 0)
        def _():
            finish(y)

        for row in (below, above, across):
            finish(row)

    halos = []

    def halo(source, target, device):
        index = len(halos)
        copy = pltpu.make_async_remote_copy(
            src_ref=source,
            dst_ref=target,
            send_sem=halo_send.at[index],
            recv_sem=halo_recv.at[index],
            device_id=device,
            device_id_type=MESH,
        )
        copy.start()
        halos.append(copy)

    def open_part(part):
        z_owner(part, start)
        ring_owner(part, start)

    open_part(0)
    for copy in last_loads:
        copy.wait()
    dequantise(1)
    open_part(1)
    dequantise(2)
    open_part(2)
    letter_load.wait()
    halo(letters.at[:, pl.ds(ROWS - 256, 256)], token_forward, after)
    halo(letters.at[:, pl.ds(0, 256)], token_backward, before)
    halo(hidden.at[pl.ds(ROWS - HALO, HALO), pl.ds(0, WIDTH)], halo_forward, after)
    halo(hidden.at[pl.ds(0, HALO), pl.ds(WIDTH, WIDTH)], halo_backward, before)

    def keep_rows(values, live):
        flags = jnp.where(values != 4, live, 0.0)
        return jnp.transpose(jnp.broadcast_to(flags, (128, 128)))

    one = jnp.float32(1.0)
    for block in range(ROWS // 128):
        keep[block * 128 + 256 : block * 128 + 384] = keep_rows(
            letters[:, block * 128 : block * 128 + 128], one
        )

    def project(values):
        wide = values.astype(F32)
        mean = jnp.mean(wide * wide, axis=-1, keepdims=True)
        return (wide * lax.rsqrt(mean + 1e-5)).astype(BF16)

    def norm_pass(part, carry):
        rows = pl.ds(pl.multiple_of(part * PART, PART), PART)
        for strand in range(2):
            start = part // 2 * (2 * TILE) + strand * TILE + part % 2 * PART
            normed[pl.ds(pl.multiple_of(start, PART), PART)] = project(state[strand, rows])
        return carry

    for copy in state_loads:
        copy.wait()
    lax.fori_loop(0, 1, norm_pass, 0)
    relay(0)
    lax.fori_loop(1, 3, norm_pass, 0)
    relay(1)
    lax.fori_loop(3, 4, norm_pass, 0)
    collect(0)
    relay(2)
    collect(1)

    for copy in filter_loads:
        copy.wait()
    short = short_filter[...].astype(F32)
    long = long_filter[...]
    padded = jnp.concatenate([short, jnp.zeros((16 - SHORT, WIDTH), F32)], axis=0).astype(BF16)
    dot = functools.partial(jnp.dot, preferred_element_type=F32)
    long_hat = dot(long_high[...], long) + dot(long_low[...], long)
    short_hat = dot(short_high[...], padded) + dot(short_low[...], padded)
    real_long, imag_long = long_hat[:BLOCK], long_hat[BLOCK:]
    real_short, imag_short = short_hat[:BLOCK], short_hat[BLOCK:]
    first = lax.broadcasted_iota(jnp.int32, (BLOCK, WIDTH), 0) == 0
    scale = jnp.where(first, 1.0 / SPAN, 2.0 / SPAN)
    reals, imags = real_short * real_long, imag_short * imag_long
    pure[...] = jnp.where(first, reals, reals - imags) * scale
    edge[...] = jnp.where(first, imags, reals - imags) * scale
    cross[...] = jnp.where(first, 0.0, real_short * imag_long + imag_short * real_long) * scale
    long_head = long[:16].astype(F32)
    taps[0:1] = short[0:1] * long_head[0:1]
    taps[1:2] = short[0:1] * long_head[1:2] + short[1:2] * long_head[0:1]

    for copy in table_loads:
        copy.wait()
    share(0)
    complete(0)

    def value_tile(tile, count):
        start = tile * TILE
        values = dot(normed[2 * start : 2 * start + count], weights[0])
        flags = jnp.tile(keep[start + 256 : start + 256 + TILE], (1, 6))
        masked_forward[start + HALO : start + HALO + TILE] = (values[:TILE] * flags).astype(BF16)
        masked_backward[start : start + TILE] = (values[TILE : 2 * TILE] * flags).astype(BF16)
        return values[2 * TILE :]

    value_tile(0, 2 * TILE)
    collect(2)
    share(1)
    for copy in halos:
        copy.wait_recv()
    live_before = jnp.where(ctx > 0, 1.0, 0.0)
    live_after = jnp.where(ctx < CTX - 1, 1.0, 0.0)
    for block in range(2):
        columns = slice(block * 128, block * 128 + 128)
        keep[columns] = keep_rows(token_forward[:, columns], live_before)
        keep[ROWS + 256 + block * 128 : ROWS + 384 + block * 128] = keep_rows(
            token_backward[:, columns], live_after
        )
    normed[2 * ROWS : 2 * ROWS + HALO] = project(halo_forward[...])
    normed[2 * ROWS + HALO :] = project(halo_backward[...])
    rims = value_tile(1, 2 * TILE + 2 * HALO)
    masked_forward[:HALO] = (rims[:HALO] * jnp.tile(keep[256 - HALO : 256], (1, 6))).astype(BF16)
    masked_backward[ROWS:] = (
        rims[HALO:] * jnp.tile(keep[ROWS + 256 : ROWS + 256 + HALO], (1, 6))
    ).astype(BF16)

    def filtered(strand, start, target):
        masked = masked_backward if strand else masked_forward
        origin = start if strand else pl.multiple_of(start + 16, 16)
        window = masked[pl.ds(origin, SPAN)]
        waves = dot(spread[...], window)
        real, imag = waves[:BLOCK], waves[BLOCK:]
        straight, turned = real * pure[...], imag * cross[...]
        upright, bent = imag * edge[...], real * cross[...]
        if strand:
            parts = [straight + turned, upright - bent]
        else:
            parts = [straight - turned, upright + bent]
        product = jnp.concatenate([part.astype(BF16) for part in parts], axis=0)
        gather = gather_backward if strand else gather_forward
        conv[target : target + BLOCK] = dot(gather[...], product)
        last, second = taps[0:1], taps[1:2]
        row = lax.broadcasted_iota(jnp.int32, (8, WIDTH), 0)
        if strand:
            wrong = masked[pl.ds(start, 16)].astype(F32)
            right = masked[pl.ds(pl.multiple_of(start + SPAN, 16), 16)].astype(F32)
            gap = right - wrong
            outer, inner = gap[0:1], gap[1:2]
            fix = jnp.where(row == 7, second * outer + last * inner, 0.0)
            fix = fix + jnp.where(row == 6, last * outer, 0.0)
            conv[target + BLOCK - 8 : target + BLOCK] += fix
        else:
            right = masked[pl.ds(start, 16)].astype(F32)
            wrong = masked[pl.ds(pl.multiple_of(start + SPAN, 16), 16)].astype(F32)
            gap = right - wrong
            outer, inner = gap[15:16], gap[14:15]
            fix = jnp.where(row == 0, second * outer + last * inner, 0.0)
            fix = fix + jnp.where(row == 1, last * outer, 0.0)
            conv[target : target + 8] += fix

    def store(tile):
        rows = pl.ds(pl.multiple_of(tile * 2 * TILE, TILE), 2 * TILE)
        return pltpu.make_async_copy(normed.at[rows], gated_out.at[rows], store_sem.at[tile])

    def conv_pass(tile, carry):
        start = pl.multiple_of(tile * TILE, TILE)
        for strand in range(2):
            for offset in range(0, TILE, BLOCK):
                filtered(strand, pl.multiple_of(start + offset, BLOCK), strand * TILE + offset)
        return carry

    def gate_pass(tile, carry):
        rows = pl.ds(pl.multiple_of(tile * 2 * TILE, TILE), 2 * TILE)
        half_gate = 0.5 * dot(normed[rows], weights[1])
        gated = (half_gate * jnp.tanh(half_gate) + half_gate) * conv[...]
        normed[rows] = gated.astype(BF16)
        store(tile).start()
        return carry

    lax.fori_loop(0, 1, conv_pass, 0)
    complete(1)
    lax.fori_loop(0, 1, gate_pass, 0)
    share(2)
    lax.fori_loop(1, ROWS // TILE, conv_pass, 0)
    complete(2)
    last_store = pltpu.make_async_copy(weights.at[2], last_weights, store_sem.at[ROWS // TILE])
    last_store.start()
    lax.fori_loop(1, ROWS // TILE, gate_pass, 0)

    for copy in halos:
        copy.wait_send()
    for part in range(3):
        z_owner(part, sent)
        ring_owner(part, sent)

        @pl.when(fetches == 1)
        def _(part=part):
            for copy in ring_copies(part):
                copy.wait_send()
            aside(part, y, 0).wait_send()
            to_mate(part, y, 0).wait_send()

        for index, row in enumerate((below, above, across)):
            aside(part, row, index + 1).wait_send()
            to_mate(part, row, index + 1).wait_send()
    for tile in range(ROWS // TILE):
        store(tile).wait()
    last_store.wait()


def finish_kernel(
    hidden, gated_source, weight_source, out, weight, gated, state, load_sem, ready_sem, store_sem
):
    def fetch(unit):
        rows = pl.ds(pl.multiple_of(unit * PART, PART), PART)
        own = pl.multiple_of(unit * 2 * PART, PART)
        loads = [pltpu.make_async_copy(hidden.at[rows], state.at[rows], ready_sem.at[unit])]
        for strand in range(2):
            start = unit // 2 * (2 * TILE) + strand * TILE + unit % 2 * PART
            loads.append(
                pltpu.make_async_copy(
                    gated_source.at[pl.ds(pl.multiple_of(start, PART), PART)],
                    gated.at[pl.ds(own + strand * PART, PART)],
                    load_sem.at[unit, strand],
                )
            )
        return *loads, pltpu.make_async_copy(state.at[rows], out.at[rows], store_sem.at[unit])

    units = ROWS // PART
    first = pltpu.make_async_copy(weight_source, weight, load_sem.at[units, 0])
    first.start()
    for unit in range(units):
        for copy in fetch(unit)[:-1]:
            copy.start()
    first.wait()

    def out_pass(unit, carry):
        rows = pl.ds(pl.multiple_of(unit * PART, PART), PART)
        own = pl.ds(pl.multiple_of(unit * 2 * PART, PART), 2 * PART)
        *loads, store = fetch(unit)
        for copy in loads:
            copy.wait()
        branch = jnp.dot(gated[own], weight[...], preferred_element_type=F32)
        for strand in range(2):
            columns = slice(strand * WIDTH, strand * WIDTH + WIDTH)
            added = branch[strand * PART : strand * PART + PART]
            state[rows, columns] = (state[rows, columns].astype(F32) + added).astype(BF16)
        store.start()
        return carry

    lax.fori_loop(0, units, out_pass, 0)
    for unit in range(units):
        fetch(unit)[-1].wait()


def shards(
    hidden_state, tokens, in_codes, in_scales, out_codes, out_scales, short_filter, long_filter
):
    window = hidden_state[0]
    anywhere = pl.BlockSpec(memory_space=pl.ANY)
    dma = pltpu.SemaphoreType.DMA
    tables = constants()
    gated, last_weights = pl.pallas_call(
        layer_kernel,
        out_shape=(
            jax.ShapeDtypeStruct((2 * ROWS, WIDTH), BF16),
            jax.ShapeDtypeStruct((WIDTH, WIDTH), BF16),
        ),
        in_specs=[anywhere] * (8 + len(tables)),
        out_specs=(anywhere, anywhere),
        scratch_shapes=[
            pltpu.VMEM((3, WIDTH, WIDTH), BF16),
            pltpu.VMEM((3, 32, 2 * WIDTH), BF16),
            pltpu.VMEM((3, 32, WIDTH), BF16),
            pltpu.VMEM((3, 12), F32),
            pltpu.VMEM((3, 6), F32),
            pltpu.VMEM((1, ROWS), jnp.int32),
            pltpu.VMEM((1, 256), jnp.int32),
            pltpu.VMEM((1, 256), jnp.int32),
            pltpu.VMEM((HALO, WIDTH), BF16),
            pltpu.VMEM((HALO, WIDTH), BF16),
            pltpu.VMEM((SHORT, WIDTH), BF16),
            pltpu.VMEM((LONG, WIDTH), BF16),
            *(pltpu.VMEM(table.shape, BF16) for table in tables),
            pltpu.VMEM((2, ROWS, WIDTH), BF16),
            pltpu.VMEM((2 * ROWS + 2 * HALO, WIDTH), BF16),
            pltpu.VMEM((ROWS + HALO, WIDTH), BF16),
            pltpu.VMEM((ROWS + HALO, WIDTH), BF16),
            pltpu.VMEM((ROWS + 512, 128), F32),
            pltpu.VMEM((BLOCK, WIDTH), F32),
            pltpu.VMEM((BLOCK, WIDTH), F32),
            pltpu.VMEM((BLOCK, WIDTH), F32),
            pltpu.VMEM((8, WIDTH), F32),
            pltpu.VMEM((2 * TILE, WIDTH), F32),
            dma((16,)),
            dma((8,)),
            dma((3, 4)),
            dma((3, 4)),
            dma((3, 4)),
            dma((4,)),
            dma((3, 2)),
            dma((3, 3)),
            dma((3, 4)),
            dma((3, 4)),
            dma((4,)),
        ],
        compiler_params=pltpu.CompilerParams(
            collective_id=0, has_side_effects=True, vmem_limit_bytes=VMEM_LIMIT
        ),
        name="layer",
    )(
        window,
        tokens,
        in_codes,
        in_scales,
        out_codes,
        out_scales,
        short_filter,
        long_filter,
        *map(jnp.asarray, tables),
    )
    result = pl.pallas_call(
        finish_kernel,
        out_shape=jax.ShapeDtypeStruct((ROWS, 2 * WIDTH), BF16),
        in_specs=[anywhere] * 3,
        out_specs=anywhere,
        scratch_shapes=[
            pltpu.VMEM((WIDTH, WIDTH), BF16),
            pltpu.VMEM((2 * ROWS, WIDTH), BF16),
            pltpu.VMEM((ROWS, 2 * WIDTH), BF16),
            dma((ROWS // PART + 1, 2)),
            dma((8,)),
            dma((8,)),
        ],
        compiler_params=pltpu.CompilerParams(vmem_limit_bytes=VMEM_LIMIT),
        name="finish",
    )(window, gated, last_weights)
    return result[None]


def solution(mesh):
    in_specs = (
        P("dp", "ctx", None),
        P("dp", "ctx"),
        P("dp", None, None),
        P("dp", None),
        P("dp", None, None),
        P("dp", None),
        P(),
        P(),
    )
    out_specs = P("dp", "ctx", None)
    return jax.shard_map(shards, mesh=mesh, in_specs=in_specs, out_specs=out_specs, check_vma=False)
```
